128 devices in a mesh: gx: 4 (over y_hi, core), gy: 4 (over x), gz: 8 (over z, y_lo).
Axes of the slice: x: 4, y: 4 (y_hi: 2, y_lo: 2; y = y_hi * 2 + y_lo), z: 4, core: 2. Of those that a mesh axis runs over, the one named last changes fastest.
Arguments:
- vol_field: float32 [8, 128, 64, 1024], P(None, 'gx', 'gy', 'gz'), may hold values from -6 to 6
- scaling: float32 [128, 64, 1024], P('gx', 'gy', 'gz'), may hold values from 0.5 to 2
- diag_shift: float32 [128, 64, 1024], P('gx', 'gy', 'gz'), may hold values from 0.5 to 2
- bnd_field: float32 [8, 16384], P(None, ('gx', 'gy', 'gz')), may hold values from -6 to 6
- bnd_cell: int32 [16384], P(('gx', 'gy', 'gz')), may hold values from 0 to 65535, as said below
- labels: int32 [16384], P(('gx', 'gy', 'gz')), may hold values from 0 to 31
- lr_left: bfloat16 [64, 64, 32, 256], P(('gx', 'gy'), 'gz'), may hold values from -1 to 1
- lr_right: bfloat16 [64, 64, 32, 256], P(('gx', 'gy'), 'gz'), may hold values from -0.046875 to 0.046875
- near_tiles: bfloat16 [64, 8, 256, 256], P(('gx', 'gy'), 'gz'), may hold values from -0.125 to 0.125
- near_slot: int32 [64, 64], P(('gx', 'gy'), 'gz'), may hold values from -1 to 0, as said below
Outputs:
- vol_out: float32 [8, 128, 64, 1024], P(None, 'gx', 'gy', 'gz')
- bnd_out: float32 [8, 16384], P(None, ('gx', 'gy', 'gz'))
- charges: float32 [32, 8], replicated
The draws below stay inside these ranges and needn't reach their ends.
Inputs may be any that keep to these rules, and one draw needn't show every extreme that they name: `bnd_cell`: within each block of 128 entries owned by one device the cells are distinct. `near_slot`: each tile row holds, within each column group of 8 tiles, exactly one near-field tile (slot 0); all other entries are -1, and the factors of near-field tiles are not used.
All inputs are finite; a program needn't handle non-finite values.
Results may differ from the reference program's by a relative error of at most 0.0003.
Values sent between devices are 32-bit elements; how exact they have to be, the bound alone decides.
A program may use at most 128 MiB of HBM per device.

```python
import math
import jax
import jax.numpy as jnp
from jax import lax

COLS = 8
CX = 32
CY = 16
CZ = 128
TB = 256
R = 32
SLOTS = 1
CONDUCTORS = 32
TILES = 64
CTD = 8
NB = 16384
BND_DEV = 128
NX = 128
NY = 64
NZ = 1024
N_GY = 4
N_GZ = 8
DEVICES = 128


def draw_bnd_cell(key, part):
    key = jax.random.fold_in(key, 11)
    cell_count = CX * CY * CZ
    pick_key, marked_key = jax.random.split(key)
    marked = jax.random.randint(marked_key, (), 0, DEVICES)
    block_keys = jax.random.split(pick_key, DEVICES)

    def draw_block(sub_key, block_index):
        perm_key, order_key = jax.random.split(sub_key)
        interior = jax.random.permutation(perm_key, cell_count - 2)[:BND_DEV].astype(jnp.int32) + 1
        with_ends = jnp.concatenate([jnp.array([0, cell_count - 1], jnp.int32), interior[:BND_DEV - 2]])
        shuffle = jax.random.permutation(order_key, BND_DEV)
        forced = with_ends[shuffle]
        return jnp.where(block_index == marked, forced, interior)
    cells = jax.vmap(draw_block)(block_keys, jnp.arange(DEVICES, dtype=jnp.int32))
    return cells.reshape(NB).astype(jnp.int32)


def draw_near_slot(key, part):
    key = jax.random.fold_in(key, 23)
    row_keys = jax.random.split(key, TILES * N_GZ)
    ranked = jax.vmap(lambda sub_key: jax.random.permutation(sub_key, CTD))(row_keys).astype(jnp.int32)
    slot_map = jnp.where(ranked < SLOTS, ranked, -1)
    return slot_map.reshape(TILES, TILES).astype(jnp.int32)


def set_ends(result, stream_key, smallest, top_value):
    shape = result.shape
    place = [jax.random.randint(jax.random.fold_in(stream_key, axis), (), 0, shape[axis]) for axis in range(len(shape))]
    result = result.at[tuple(place)].set(smallest)
    longest = shape.index(max(shape))
    place[longest] = (place[longest] + 1) % shape[longest]
    return result.at[tuple(place)].set(top_value)


def block_levels(key, dims, pieces, low, top_value):
    factor_of, own = 1.0, jax.random.fold_in(key, 6)
    for dim, blocks in pieces:
        draws = jnp.exp(jax.random.uniform(jax.random.fold_in(own, dim), (blocks,), jnp.float32, low / len(pieces), top_value / len(pieces)))
        factor_of = factor_of * jnp.repeat(draws, dims[dim] // blocks).reshape([-1 if axis == dim else 1 for axis in range(len(dims))])
    return factor_of


def centred(rng, extent, scale, limit, cuts=(), kind=jnp.bfloat16):
    factor_of = block_levels(rng, extent, cuts, -0.22, 0.18) if cuts else 1.0
    drawn = jax.random.normal(rng, extent, jnp.float32) * scale * factor_of
    return jnp.minimum(jnp.maximum(drawn, -limit), limit).astype(kind)


def setup_inputs(seed: int = 0) -> dict:
    streams_of = jax.random.split(jax.random.key(seed), 11)
    vol_field = centred(streams_of[0], (COLS, NX, NY, NZ), 1.0, 6.0, ((1, 4), (2, 4), (3, 8)), jnp.float32)
    scaling = jnp.clip(jnp.exp(math.log(2.0) - 1.3862944 * jax.random.uniform(streams_of[1], (NX, NY, NZ), jnp.float32) ** block_levels(streams_of[1], (NX, NY, NZ), ((0, 4), (1, 4), (2, 8)), -0.2, 0.2)), 0.5, 2.0)
    diag_shift = jnp.clip(jnp.exp(math.log(2.0) - 1.3862944 * jax.random.uniform(streams_of[2], (NX, NY, NZ), jnp.float32) ** block_levels(streams_of[2], (NX, NY, NZ), ((0, 4), (1, 4), (2, 8)), -0.2, 0.2)), 0.5, 2.0)
    bnd_field = centred(streams_of[3], (COLS, NB), 1.0, 6.0, ((1, 128),), jnp.float32)
    bnd_cell = draw_bnd_cell(jax.random.fold_in(streams_of[10], 71), 0)
    labels = set_ends(jax.random.randint(streams_of[5], (NB,), 0, CONDUCTORS), jax.random.fold_in(streams_of[5], 1), 0, CONDUCTORS - 1).astype(jnp.int32)
    lr_left = centred(streams_of[6], (TILES, TILES, R, TB), R ** -0.5, 1.0, ((0, 16), (1, 8)))
    lr_right = centred(streams_of[7], (TILES, TILES, R, TB), NB ** -0.5, 0.046875, ((0, 16), (1, 8)))
    near_tiles = centred(streams_of[8], (TILES, N_GZ * SLOTS, TB, TB), (N_GZ * SLOTS * TB) ** -0.5, 0.125, ((0, 16), (1, 8)))
    near_slot = draw_near_slot(jax.random.fold_in(streams_of[10], 71), 0)
    return {"vol_field": vol_field, "scaling": scaling, "diag_shift": diag_shift, "bnd_field": bnd_field, "bnd_cell": bnd_cell, "labels": labels, "lr_left": lr_left, "lr_right": lr_right, "near_tiles": near_tiles, "near_slot": near_slot}


HIGHEST = lax.Precision.HIGHEST


def apply_line(values, axis_dim, use_mass):
    length = values.shape[axis_dim]
    lower_cells = lax.slice_in_dim(values, 0, length - 2, axis=axis_dim)
    middle = lax.slice_in_dim(values, 1, length - 1, axis=axis_dim)
    upper_cells = lax.slice_in_dim(values, 2, length, axis=axis_dim)
    if use_mass:
        return (lower_cells + 4.0 * middle + upper_cells) / 6.0
    return 2.0 * middle - lower_cells - upper_cells


def stiffness(one_column):
    padded = jnp.pad(one_column, 1)
    mass_x = apply_line(padded, 0, True)
    stiff_x = apply_line(padded, 0, False)
    mass_xy = apply_line(mass_x, 1, True)
    stiff_xy = apply_line(mass_x, 1, False) + apply_line(stiff_x, 1, True)
    return apply_line(stiff_xy, 2, True) + apply_line(mass_xy, 2, False)


def reference(vol_field, scaling, diag_shift, bnd_field, bnd_cell, labels, lr_left, lr_right, near_tiles, near_slot):
    def column_out(one_column):
        return scaling * stiffness(scaling * one_column) + diag_shift * one_column

    vol_base = lax.map(column_out, vol_field)
    owner_id = jnp.arange(NB, dtype=jnp.int32) // BND_DEV
    owner_x = owner_id // (N_GY * N_GZ)
    owner_y = (owner_id // N_GZ) % N_GY
    owner_z = owner_id % N_GZ
    local_x = bnd_cell // (CY * CZ)
    local_y = (bnd_cell // CZ) % CY
    local_z = bnd_cell % CZ
    flat_index = ((owner_x * CX + local_x) * NY + owner_y * CY + local_y) * NZ + owner_z * CZ + local_z
    flat_index = flat_index.astype(jnp.int32)
    traced_vol = vol_field.reshape(COLS, NX * NY * NZ)[:, flat_index]
    vol_out = vol_base.reshape(COLS, NX * NY * NZ).at[:, flat_index].add(bnd_field).reshape(COLS, NX, NY, NZ)

    x_tiles = bnd_field.reshape(COLS, TILES, TB)
    far_mask = (near_slot < 0).astype(jnp.float32)
    projected = jnp.einsum("ijrt,cjt->ijrc", lr_right.astype(jnp.float32), x_tiles, precision=HIGHEST)
    projected = projected * far_mask[:, :, None, None]
    far_field = jnp.einsum("ijrt,ijrc->cit", lr_left.astype(jnp.float32), projected, precision=HIGHEST)
    group_slot = near_slot.reshape(TILES, N_GZ, CTD)
    picked = (group_slot[:, :, :, None] == jnp.arange(SLOTS, dtype=jnp.int32)[None, None, None, :]).astype(jnp.float32)
    x_groups = bnd_field.reshape(COLS, N_GZ, CTD, TB)
    chosen = jnp.einsum("igjs,cgju->igscu", picked, x_groups, precision=HIGHEST)
    near_group = near_tiles.reshape(TILES, N_GZ, SLOTS, TB, TB).astype(jnp.float32)
    near_field = jnp.einsum("igstu,igscu->cit", near_group, chosen, precision=HIGHEST)
    applied = (far_field + near_field).reshape(COLS, NB)
    bnd_out = traced_vol - applied
    charges = jax.ops.segment_sum(bnd_out.T, labels, num_segments=CONDUCTORS) * (CONDUCTORS / NB) ** 0.5
    return vol_out, bnd_out, charges
```

```python
import functools

import jax
import jax.numpy as jnp
from jax import lax
from jax.experimental import pallas as pl
from jax.experimental.pallas import tpu as pltpu
from jax.sharding import PartitionSpec as P

MESH = pl.DeviceIdType.MESH
F32 = jnp.float32
BF16 = jnp.bfloat16

NX, NY, NZ = 4, 4, 8
PEERS = NX * NY
COLS, CX, CY, CZ = 8, 32, 16, 128
ROWS, TILES, RANK, TB = 4, 8, 32, 256
CONDUCTORS = 32
BND = 128
GROUP = PEERS
NEIGHBOURS = [(dx, dy) for dx in (-1, 0, 1) for dy in (-1, 0, 1) if (dx, dy) != (0, 0)]


def split(x):
    hi = x.astype(BF16).astype(F32)
    return hi, x - hi


def stacked(x):
    hi, lo = split(x)
    return jnp.concatenate([hi, lo], axis=0).astype(BF16)


def dot(a, b):
    return lax.dot_general(a, b, (((1,), (0,)), ((), ())), preferred_element_type=F32)


def dot_nt(a, b):
    return lax.dot_general(a, b, (((1,), (1,)), ((), ())), preferred_element_type=F32)


def face(step, size):
    if step == 0:
        return pl.ds(1, size), pl.ds(1, size)
    return (pl.ds(size, 1), pl.ds(0, 1)) if step > 0 else (pl.ds(1, 1), pl.ds(size + 1, 1))


def kernel(
    vol, scal, diag, bnd, cell, lab, left, right, near, slot,
    out, bnd_out, charges,
    vbuf, wbuf, tbuf, qbuf, obuf, sbuf, dbuf, bbuf, cellv, cells, labv, slots, leftb, rightb, nearb,
    xbuf, lbuf, ohz, pbuf, mbuf, rbuf, c1, c2, zsend, zlo, zhi, zcomb, trbuf,
    load_sem, vol_sem, out_sem, xs_sem, xr_sem, ls_sem, lr_sem, hs_sem, hr_sem,
    ms_sem, mr_sem, zs_sem, zr_sem, cs_sem, cr_sem,
):
    gx, gy, gz = lax.axis_index("gx"), lax.axis_index("gy"), lax.axis_index("gz")
    me2 = gx * NY + gy
    group = me2 // 2
    pos = lax.rem(gy, 2) * NZ + gz
    lane = lax.broadcasted_iota(jnp.int32, (COLS, CZ), 1)

    small = [(bnd, bbuf), (lab, labv), (cell, cells), (cell, cellv), (slot, slots),
             (scal, sbuf), (diag, dbuf), (right, rightb), (left, leftb), (near, nearb)]
    loads = [pltpu.make_async_copy(s, d, load_sem.at[i]) for i, (s, d) in enumerate(small)]
    (l_bnd, l_lab, l_cells, l_cellv, l_slot, l_scal, l_diag, l_right, l_left, l_near) = loads
    for l in (l_bnd, l_lab, l_scal):
        l.start()
    for c in range(COLS):
        pltpu.make_async_copy(vol.at[c], vbuf.at[:, c, :], vol_sem).start()
    for l in (l_cells, l_cellv, l_slot, l_right, l_left, l_near, l_diag):
        l.start()

    zero = jnp.zeros((COLS, CZ), F32)
    for x in (0, CX + 1):
        wbuf[x] = jnp.zeros((CY + 2, COLS, CZ), F32)
    for y in (0, CY + 1):
        wbuf[:, y] = jnp.zeros((CX + 2, COLS, CZ), F32)
    zlo[...] = jnp.zeros_like(zlo)
    zhi[...] = jnp.zeros_like(zhi)

    barrier = pltpu.get_barrier_semaphore()
    own_group = group == gz

    def greet(device):
        pl.semaphore_signal(barrier, inc=1, device_id=device, device_id_type=MESH)

    for p in range(GROUP):
        source = (gz // 2, lax.rem(gz, 2) * 2 + p // NZ, p % NZ)
        pl.when(jnp.logical_not(jnp.logical_and(own_group, pos == p)))(functools.partial(greet, source))
    for d in range(1, NZ):
        greet((gx, gy, lax.rem(gz + d, NZ)))
    for e in range(1, PEERS):
        other = lax.rem(me2 + e, PEERS)
        greet((other // NY, lax.rem(other, NY), gz))
    own = own_group.astype(jnp.int32)

    l_bnd.wait()
    l_lab.wait()
    pl.semaphore_wait(barrier, GROUP - own + (NZ - 1) + (PEERS - 1))

    def x_copy(t):
        return pltpu.make_async_remote_copy(
            bbuf, xbuf.at[pos], xs_sem.at[t], xr_sem,
            device_id=(t // NY, t % NY, group), device_id_type=MESH)

    x_self = pltpu.make_async_copy(bbuf, xbuf.at[pos], xr_sem)
    for t in range(GROUP):
        mine = jnp.logical_and(own_group, me2 == t)
        pl.when(jnp.logical_not(mine))(lambda t=t: x_copy(t).start())
    pl.when(own_group)(lambda: x_self.start())
    lbuf[gz] = labv[...]
    label_sends = [
        pltpu.make_async_remote_copy(
            labv, lbuf.at[gz], ls_sem, lr_sem,
            device_id=(gx, gy, lax.rem(gz + d, NZ)), device_id_type=MESH)
        for d in range(1, NZ)]
    for s in label_sends:
        s.start()

    l_scal.wait()
    pltpu.make_async_copy(vbuf, vbuf, vol_sem).wait()

    @pl.loop(0, CX)
    def _(x):
        for y in range(CY):
            s = sbuf[x, pl.ds(y, 1), :] * (1.0 / 6.0)
            wbuf[x + 1, y + 1] = jnp.broadcast_to(s, (COLS, CZ)) * vbuf[x * CY + y]

    halo = []
    for i, (dx, dy) in enumerate(NEIGHBOURS):
        (fx, tx), (fy, ty) = face(dx, CX), face(dy, CY)
        copy = pltpu.make_async_remote_copy(
            wbuf.at[fx, fy], wbuf.at[tx, ty], hs_sem.at[i], hr_sem.at[i],
            device_id=(lax.rem(gx + dx + NX, NX), lax.rem(gy + dy + NY, NY), gz), device_id_type=MESH)

        def within(a, b):
            return jnp.logical_and(jnp.logical_and(a >= 0, a < NX), jnp.logical_and(b >= 0, b < NY))

        to, come = within(gx + dx, gy + dy), within(gx - dx, gy - dy)
        pl.when(to)(copy.start)
        halo.append((copy, to, come))

    l_cells.wait()
    l_cellv.wait()

    def trace_one(k, acc):
        place = cells[0, k]
        row = vbuf[lax.shift_right_logical(place, 7)]
        turn = jnp.bitwise_and(k + CZ - jnp.bitwise_and(place, CZ - 1), CZ - 1)
        return jnp.where(lane == k, pltpu.roll(row, turn, 1), acc)

    traced = lax.fori_loop(0, BND, trace_one, zero, unroll=8)
    trbuf[...] = traced

    node = cellv[...]
    zk = jnp.bitwise_and(node, CZ - 1)
    onehot = (lax.broadcasted_iota(jnp.int32, (CZ, BND), 0) == zk).astype(F32).astype(BF16)
    ohz[:, pl.ds(0, BND)] = onehot
    ohz[:, pl.ds(BND, BND)] = onehot

    l_slot.wait()
    l_right.wait()
    l_left.wait()
    l_near.wait()
    pltpu.make_async_copy(xbuf, xbuf, xr_sem).wait()
    pieces = []
    for j in range(TILES):
        xj = jnp.concatenate([xbuf[2 * j], xbuf[2 * j + 1]], axis=1)
        hi, lo = split(xj)
        pieces.append(jnp.concatenate([hi, lo], axis=0))
    xall = jnp.concatenate(pieces, axis=0).astype(BF16)
    lane2 = lax.broadcasted_iota(jnp.int32, (COLS, TB), 1)
    for i in range(ROWS):
        proj = dot_nt(xall, rightb[i])
        acc = jnp.zeros((COLS, TB), F32)
        chosen = jnp.zeros((2 * COLS, TB), F32)
        for j in range(TILES):
            is_far = slots[i, j] < 0
            far = jnp.where(is_far, 1.0, 0.0).astype(F32)
            block = proj[16 * j:16 * j + 8] + proj[16 * j + 8:16 * j + 16]
            acc = jnp.where(lane2 // RANK == j, block * far, acc)
            chosen = chosen + pieces[j] * (1.0 - far)
        both = dot(stacked(acc), leftb[i]) + dot_nt(chosen.astype(BF16), nearb[i])
        part = -(both[:COLS] + both[COLS:])
        pbuf[2 * i] = part[:, :BND]
        pbuf[2 * i + 1] = part[:, BND:]

    pltpu.make_async_copy(lbuf.at[pl.ds(0, NZ - 1)], lbuf.at[pl.ds(0, NZ - 1)], lr_sem).wait()
    which = lax.broadcasted_iota(jnp.int32, (CONDUCTORS, BND), 0)

    def members(labels):
        return (which == labels).astype(F32).astype(BF16)

    gathered = dot_nt(stacked(trbuf[...]), members(labv[...]))
    for b in range(NZ):
        gathered = gathered + dot_nt(stacked(pbuf[b]), members(lbuf[b]))
    sums = jnp.concatenate([gathered[:COLS] + gathered[COLS:], jnp.zeros((COLS, BND - CONDUCTORS), F32)], axis=1)
    for b in range(NZ):
        mbuf[b, pl.ds(0, COLS), :] = pbuf[b]
        mbuf[b, pl.ds(COLS, COLS), :] = sums

    row_sends = []
    for d in range(1, NZ):
        other = lax.rem(gz + d, NZ)
        row_sends.append(pltpu.make_async_remote_copy(
            mbuf.at[other], rbuf.at[gz], ms_sem, mr_sem,
            device_id=(gx, gy, other), device_id_type=MESH))
    for s in row_sends:
        s.start()
    rbuf[gz] = mbuf[gz]

    for copy, to, come in halo:
        pl.when(come)(copy.wait_recv)

    @pl.loop(0, CX)
    def _(x):
        a = [wbuf[x, y] + wbuf[x + 2, y] for y in range(CY + 2)]
        w = [wbuf[x + 1, y] for y in range(CY + 2)]
        packed = zero
        for y in range(CY):
            p = a[y] + a[y + 2]
            t = (a[y + 1] + (w[y] + w[y + 2])) + 0.5 * p
            tbuf[x * CY + y] = t
            qbuf[x * CY + y] = 16.0 * w[y + 1] - p
            ends = jnp.logical_or(lane == (2 * y + CZ - 1) % CZ, lane == 2 * y)
            packed = jnp.where(ends, pltpu.roll(t, 2 * y, 1) if y else t, packed)
        quarter = lax.rem(x, 4)
        packed = pltpu.roll(packed, quarter * (2 * CY), 1)
        window = jnp.bitwise_and(lane + 1, CZ - 1) // (2 * CY) == quarter
        zsend[x // 4] = jnp.where(window, packed, zsend[x // 4])

    up, down = gz + 1 < NZ, gz > 0
    z_up = pltpu.make_async_remote_copy(
        zsend, zlo, zs_sem.at[0], zr_sem.at[0],
        device_id=(gx, gy, lax.rem(gz + 1, NZ)), device_id_type=MESH)
    z_down = pltpu.make_async_remote_copy(
        zsend, zhi, zs_sem.at[1], zr_sem.at[1],
        device_id=(gx, gy, lax.rem(gz + NZ - 1, NZ)), device_id_type=MESH)
    pl.when(up)(z_up.start)
    pl.when(down)(z_down.start)

    pltpu.make_async_copy(rbuf.at[pl.ds(0, NZ - 1)], rbuf.at[pl.ds(0, NZ - 1)], mr_sem).wait()
    total = rbuf[0]
    for b in range(1, NZ):
        total = total + rbuf[b]
    bnd_out[...] = trbuf[...] + total[:COLS]
    c1[...] = total[COLS:]
    c_sends = []
    for e in range(1, PEERS):
        other = lax.rem(me2 + e, PEERS)
        c_sends.append(pltpu.make_async_remote_copy(
            c1, c2.at[me2], cs_sem, cr_sem,
            device_id=(other // NY, lax.rem(other, NY), gz), device_id_type=MESH))
    for s in c_sends:
        s.start()
    c2[me2] = c1[...]

    l_diag.wait()
    pl.when(down)(z_up.wait_recv)
    pl.when(up)(z_down.wait_recv)
    odd = jnp.bitwise_and(lane, 1) == 1
    for g in range(CX // 4):
        zcomb[g] = jnp.where(odd, pltpu.roll(zlo[g], 2, 1), zhi[g])
    spots = jnp.broadcast_to(lax.shift_right_logical(node, 7), (COLS, BND))
    bhi, blo = split(bbuf[...])

    def second(x):
        rows = []
        for y in range(CY):
            here = spots == x * CY + y
            rows.append(jnp.concatenate([jnp.where(here, bhi, 0.0), jnp.where(here, blo, 0.0)], axis=1))
        extra = dot_nt(jnp.concatenate(rows, axis=0).astype(BF16), ohz[...])
        ends = pltpu.roll(zcomb[x // 4], lax.rem(4 - lax.rem(x, 4), 4) * (2 * CY), 1)
        for y in range(CY):
            t = tbuf[x * CY + y]
            r = pltpu.roll(ends, CZ - (2 * y + 1), 1)
            nb = jnp.where(lane == 0, r, pltpu.roll(t, 1, 1)) + jnp.where(lane == CZ - 1, r, pltpu.roll(t, CZ - 1, 1))
            s = jnp.broadcast_to(sbuf[x, pl.ds(y, 1), :], (COLS, CZ))
            d = jnp.broadcast_to(dbuf[x, pl.ds(y, 1), :], (COLS, CZ))
            base = s * (qbuf[x * CY + y] - nb) + d * vbuf[x * CY + y]
            obuf[x * CY + y] = base + extra[COLS * y:COLS * (y + 1)]

    chunk = 8
    for k in range(CX // chunk):
        pl.loop(k * chunk, (k + 1) * chunk)(second)
        rows = pl.ds(k * chunk * CY, chunk * CY)
        for c in range(COLS):
            pltpu.make_async_copy(obuf.at[rows, c, :], out.at[c, rows, :], out_sem).start()

    pltpu.make_async_copy(c2.at[pl.ds(0, PEERS - 1)], c2.at[pl.ds(0, PEERS - 1)], cr_sem).wait()
    total = c2[0]
    for b in range(1, PEERS):
        total = total + c2[b]
    charges[...] = total[:, :CONDUCTORS] * (CONDUCTORS / (BND * NX * NY * NZ)) ** 0.5

    for t in range(GROUP):
        mine = jnp.logical_and(own_group, me2 == t)
        pl.when(jnp.logical_not(mine))(lambda t=t: x_copy(t).wait_send())
    for s in label_sends + row_sends + c_sends:
        s.wait_send()
    for copy, to, come in halo:
        pl.when(to)(copy.wait_send)
    pl.when(up)(z_up.wait_send)
    pl.when(down)(z_down.wait_send)
    pltpu.make_async_copy(obuf, obuf, out_sem).wait()


def shards(vol, scal, diag, bnd, cell, lab, left, right, near, slot):
    any_spec = pl.BlockSpec(memory_space=pl.ANY)
    vmem_spec = pl.BlockSpec(memory_space=pltpu.VMEM)
    nodes = CX * CY
    field = (nodes, COLS, CZ)
    dma = pltpu.SemaphoreType.DMA
    out, bnd_out, charges = pl.pallas_call(
        kernel,
        out_shape=(
            jax.ShapeDtypeStruct((COLS, nodes, CZ), F32),
            jax.ShapeDtypeStruct((COLS, BND), F32),
            jax.ShapeDtypeStruct((COLS, CONDUCTORS), F32),
        ),
        in_specs=[any_spec] * 10,
        out_specs=(any_spec, vmem_spec, vmem_spec),
        scratch_shapes=[
            pltpu.VMEM(field, F32),
            pltpu.VMEM((CX + 2, CY + 2, COLS, CZ), F32),
            pltpu.VMEM(field, F32),
            pltpu.VMEM(field, F32),
            pltpu.VMEM(field, F32),
            pltpu.VMEM((CX, CY, CZ), F32),
            pltpu.VMEM((CX, CY, CZ), F32),
            pltpu.VMEM((COLS, BND), F32),
            pltpu.VMEM((1, BND), jnp.int32),
            pltpu.SMEM((1, BND), jnp.int32),
            pltpu.VMEM((1, BND), jnp.int32),
            pltpu.SMEM((ROWS, TILES), jnp.int32),
            pltpu.VMEM((ROWS, TB, TB), BF16),
            pltpu.VMEM((ROWS, TB, TB), BF16),
            pltpu.VMEM((ROWS, TB, TB), BF16),
            pltpu.VMEM((GROUP, COLS, BND), F32),
            pltpu.VMEM((NZ, 1, BND), jnp.int32),
            pltpu.VMEM((CZ, 2 * BND), BF16),
            pltpu.VMEM((NZ, COLS, BND), F32),
            pltpu.VMEM((NZ, 2 * COLS, BND), F32),
            pltpu.VMEM((NZ, 2 * COLS, BND), F32),
            pltpu.VMEM((COLS, BND), F32),
            pltpu.VMEM((PEERS, COLS, BND), F32),
            pltpu.VMEM((CX // 4, COLS, CZ), F32),
            pltpu.VMEM((CX // 4, COLS, CZ), F32),
            pltpu.VMEM((CX // 4, COLS, CZ), F32),
            pltpu.VMEM((CX // 4, COLS, CZ), F32),
            pltpu.VMEM((COLS, BND), F32),
            dma((10,)), dma, dma, dma((GROUP,)), dma, dma, dma, dma((8,)), dma((8,)),
            dma, dma, dma((2,)), dma((2,)), dma, dma,
        ],
        compiler_params=pltpu.CompilerParams(
            collective_id=0, has_side_effects=True, vmem_limit_bytes=40 * 1024 * 1024),
    )(
        vol.reshape(COLS, nodes, CZ), scal, diag, bnd, cell.reshape(1, BND), lab.reshape(1, BND),
        left.reshape(ROWS, TB, TB), right.reshape(ROWS, TB, TB), near.reshape(ROWS, TB, TB), slot,
    )
    return out.reshape(vol.shape), bnd_out, charges.T


def solution(mesh):
    in_specs = (
        P(None, "gx", "gy", "gz"),
        P("gx", "gy", "gz"),
        P("gx", "gy", "gz"),
        P(None, ("gx", "gy", "gz")),
        P(("gx", "gy", "gz")),
        P(("gx", "gy", "gz")),
        P(("gx", "gy"), "gz", None, None),
        P(("gx", "gy"), "gz", None, None),
        P(("gx", "gy"), "gz", None, None),
        P(("gx", "gy"), "gz"),
    )
    out_specs = (P(None, "gx", "gy", "gz"), P(None, ("gx", "gy", "gz")), P())
    return jax.shard_map(shards, mesh=mesh, in_specs=in_specs, out_specs=out_specs, check_vma=False)
```

```python
import functools

import jax
import jax.numpy as jnp
from jax import lax
from jax.experimental import pallas as pl
from jax.experimental.pallas import tpu as pltpu
from jax.sharding import PartitionSpec as P

MESH = pl.DeviceIdType.MESH
F32 = jnp.float32
BF16 = jnp.bfloat16

NX, NY, NZ = 4, 4, 8
PEERS = NX * NY
COLS, CX, CY, CZ = 8, 32, 16, 128
ROWS, TILES, RANK, TB = 4, 8, 32, 256
CONDUCTORS = 32
BND = 128
GROUP = PEERS
NEIGHBOURS = [(dx, dy) for dx in (-1, 0, 1) for dy in (-1, 0, 1) if (dx, dy) != (0, 0)]


def split(x):
    hi = x.astype(BF16).astype(F32)
    return hi, x - hi


def stacked(x):
    hi, lo = split(x)
    return jnp.concatenate([hi, lo], axis=0).astype(BF16)


def dot(a, b):
    return lax.dot_general(a, b, (((1,), (0,)), ((), ())), preferred_element_type=F32)


def dot_nt(a, b):
    return lax.dot_general(a, b, (((1,), (1,)), ((), ())), preferred_element_type=F32)


def face(step, size):
    if step == 0:
        return pl.ds(1, size), pl.ds(1, size)
    return (pl.ds(size, 1), pl.ds(0, 1)) if step > 0 else (pl.ds(1, 1), pl.ds(size + 1, 1))


GX = 8


def scale_pass(sbuf, vbuf, wbuf):
    @pl.loop(0, CX)
    def _(x):
        for y in range(CY):
            s = sbuf[x, pl.ds(y, 1), :] * (1.0 / 6.0)
            wbuf[x + 1, y + 1] = jnp.broadcast_to(s, (COLS, CZ)) * vbuf[x * CY + y]


def line_weights(wz, ez):
    z = lax.broadcasted_iota(jnp.int32, (CZ, CZ), 0)
    n = lax.broadcasted_iota(jnp.int32, (CZ, CZ), 1)
    near = jnp.logical_or(z == n + 1, z == n - 1)
    first = jnp.bitwise_and(n, CX) == 0
    ends = jnp.logical_or(jnp.logical_and(z == 0, first), jnp.logical_and(z == CZ - 1, jnp.logical_not(first)))
    from_above = jnp.bitwise_and(z, CX) == 0
    land = jnp.logical_or(jnp.logical_and(n == CZ - 1, from_above), jnp.logical_and(n == 0, jnp.logical_not(from_above)))

    def ones(mask):
        return mask.astype(F32).astype(BF16)

    for piece in range(2):
        rows = pl.ds(piece * CZ, CZ)
        wz[rows, pl.ds(0, CZ)] = ones(near)
        wz[rows, pl.ds(CZ, CZ)] = ones(ends)
        ez[rows, :] = ones(land)


def node_columns(cellv, ohz):
    zk = jnp.bitwise_and(cellv[...], CZ - 1)
    onehot = (lax.broadcasted_iota(jnp.int32, (CZ, BND), 0) == zk).astype(F32).astype(BF16)
    ohz[:, pl.ds(0, BND)] = onehot
    ohz[:, pl.ds(BND, BND)] = onehot


def node_pass(bbuf, cellv, ohz, vbuf, dbuf, lhs, obuf):
    spots = jnp.broadcast_to(lax.shift_right_logical(cellv[...], 7), (COLS, BND))
    pieces = split(bbuf[...])

    @pl.loop(0, CX)
    def _(x):
        for y in range(0, CY, 2):
            here = [spots == x * CY + y, spots == x * CY + y + 1]
            for p in range(2):
                both = jnp.concatenate([jnp.where(h, pieces[p], 0.0) for h in here], axis=0)
                lhs[x, pl.ds(COLS * y, 2 * COLS), pl.ds(p * BND, BND)] = both.astype(BF16)

    @pl.loop(0, CX // GX)
    def _(g):
        extra = dot_nt(lhs[pl.ds(g * GX, GX)].reshape(GX * CY * COLS, 2 * BND), ohz[...])
        for i in range(GX):
            for y in range(CY):
                x = g * GX + i
                d = jnp.broadcast_to(dbuf[x, pl.ds(y, 1), :], (COLS, CZ))
                k = (i * CY + y) * COLS
                obuf[x * CY + y] = d * vbuf[x * CY + y] + extra[k:k + COLS]


def line_pass(wbuf, lhs, qbuf):
    @pl.loop(0, CX)
    def _(x):
        a = [wbuf[x, y] + wbuf[x + 2, y] for y in range(CY + 2)]
        w = [wbuf[x + 1, y] for y in range(CY + 2)]
        for y0 in range(0, CY, 2):
            ts = []
            for y in (y0, y0 + 1):
                p = a[y] + a[y + 2]
                ts.append((a[y + 1] + (w[y] + w[y + 2])) + 0.5 * p)
                qbuf[x * CY + y] = 16.0 * w[y + 1] - p
            t = jnp.concatenate(ts, axis=0)
            hi = t.astype(BF16)
            lhs[x, pl.ds(COLS * y0, 2 * COLS), pl.ds(0, CZ)] = hi
            lhs[x, pl.ds(COLS * y0, 2 * COLS), pl.ds(CZ, CZ)] = (t - hi.astype(F32)).astype(BF16)


def sum_pass(lhs, wz, qbuf, sbuf, obuf, zsend, lane):
    spot = jnp.bitwise_and(lane, CX - 1)
    half = lax.shift_right_logical(lane, 6)

    @pl.loop(0, CX // GX)
    def _(g):
        r = dot(lhs[pl.ds(g * GX, GX)].reshape(GX * CY * COLS, 2 * CZ), wz[...])
        ends = [zsend[y] for y in range(CY // 2)]
        for i in range(GX):
            x = g * GX + i
            mine = [jnp.logical_and(half == h, spot == x) for h in range(2)]
            for y in range(CY):
                k = (i * CY + y) * COLS
                s = jnp.broadcast_to(sbuf[x, pl.ds(y, 1), :], (COLS, CZ))
                obuf[x * CY + y] = obuf[x * CY + y] + s * (qbuf[x * CY + y] - r[k:k + COLS, :CZ])
                e = y % (CY // 2)
                ends[e] = jnp.where(mine[y // (CY // 2)], r[k:k + COLS, CZ:], ends[e])
        for y in range(CY // 2):
            zsend[y] = ends[y]


def end_rows(zlo, zhi, zc, lane):
    above = jnp.bitwise_and(lane, CX) == 0
    for y in range(0, CY, 2):
        e = y % (CY // 2)
        both = []
        for k in (e, e + 1):
            row = jnp.where(above, zhi[k], zlo[k])
            both.append(jnp.where(lax.shift_right_logical(lane, 6) == y // (CY // 2), row, 0.0))
        z = jnp.concatenate(both, axis=0)
        hi = z.astype(BF16)
        zc[pl.ds(COLS * y, 2 * COLS), pl.ds(0, CZ)] = hi
        zc[pl.ds(COLS * y, 2 * COLS), pl.ds(CZ, CZ)] = (z - hi.astype(F32)).astype(BF16)


def end_pass(k, chunk, zc, ez, sbuf, obuf):
    lane2 = jnp.bitwise_and(lax.broadcasted_iota(jnp.int32, (2 * COLS, 2 * CZ), 1), CX - 1)

    @pl.loop(k * (chunk // GX), (k + 1) * (chunk // GX))
    def _(g):
        rows = []
        for i in range(GX):
            here = (lane2 == g * GX + i).astype(F32).astype(BF16)
            for y in range(0, CY, 2):
                rows.append(zc[pl.ds(COLS * y, 2 * COLS), :] * here)
        h = dot(jnp.concatenate(rows, axis=0), ez[...])
        for i in range(GX):
            x = g * GX + i
            for y in range(CY):
                q = (i * CY + y) * COLS
                s = jnp.broadcast_to(sbuf[x, pl.ds(y, 1), :], (COLS, CZ))
                obuf[x * CY + y] = obuf[x * CY + y] - s * h[q:q + COLS]


def trace_nodes(cells, vbuf, lane):
    def trace_one(k, acc):
        place = cells[0, k]
        row = vbuf[lax.shift_right_logical(place, 7)]
        turn = jnp.bitwise_and(k + CZ - jnp.bitwise_and(place, CZ - 1), CZ - 1)
        return jnp.where(lane == k, pltpu.roll(row, turn, 1), acc)

    return lax.fori_loop(0, BND, trace_one, jnp.zeros((COLS, CZ), F32), unroll=8)


def tile_products(xbuf, slots, rightb, leftb, nearb, pbuf):
    pieces = []
    for j in range(TILES):
        xj = jnp.concatenate([xbuf[2 * j], xbuf[2 * j + 1]], axis=1)
        hi, lo = split(xj)
        pieces.append(jnp.concatenate([hi, lo], axis=0))
    xall = jnp.concatenate(pieces, axis=0).astype(BF16)
    lane2 = lax.broadcasted_iota(jnp.int32, (COLS, TB), 1)
    for i in range(ROWS):
        proj = dot_nt(xall, rightb[i])
        acc = jnp.zeros((COLS, TB), F32)
        chosen = jnp.zeros((2 * COLS, TB), F32)
        for j in range(TILES):
            is_far = slots[i, j] < 0
            far = jnp.where(is_far, 1.0, 0.0).astype(F32)
            block = proj[16 * j:16 * j + 8] + proj[16 * j + 8:16 * j + 16]
            acc = jnp.where(lane2 // RANK == j, block * far, acc)
            chosen = chosen + pieces[j] * (1.0 - far)
        both = dot(stacked(acc), leftb[i]) + dot_nt(chosen.astype(BF16), nearb[i])
        part = -(both[:COLS] + both[COLS:])
        pbuf[2 * i] = part[:, :BND]
        pbuf[2 * i + 1] = part[:, BND:]


def conductor_sums(trbuf, labv, lbuf, pbuf, mbuf):
    which = lax.broadcasted_iota(jnp.int32, (CONDUCTORS, BND), 0)

    def members(labels):
        return (which == labels).astype(F32).astype(BF16)

    gathered = dot_nt(stacked(trbuf[...]), members(labv[...]))
    for b in range(NZ):
        gathered = gathered + dot_nt(stacked(pbuf[b]), members(lbuf[b]))
    sums = jnp.concatenate([gathered[:COLS] + gathered[COLS:], jnp.zeros((COLS, BND - CONDUCTORS), F32)], axis=1)
    for b in range(NZ):
        mbuf[b, pl.ds(0, COLS), :] = pbuf[b]
        mbuf[b, pl.ds(COLS, COLS), :] = sums


def kernel(
    vol, scal, diag, bnd, cell, lab, left, right, near, slot,
    obuf, bnd_out, charges,
    vbuf, wbuf, qbuf, lhs, sbuf, dbuf, bbuf, cellv, cells, labv, slots, leftb, rightb, nearb,
    xbuf, lbuf, ohz, wz, ez, zc, pbuf, mbuf, rbuf, c1, c2, zsend, zlo, zhi, trbuf,
    load_sem, vol_sem, xs_sem, xr_sem, ls_sem, lr_sem, hs_sem, hr_sem,
    ms_sem, mr_sem, zs_sem, zr_sem, cs_sem, cr_sem,
):
    gx, gy, gz = lax.axis_index("gx"), lax.axis_index("gy"), lax.axis_index("gz")
    me2 = gx * NY + gy
    group = me2 // 2
    pos = lax.rem(gy, 2) * NZ + gz
    lane = lax.broadcasted_iota(jnp.int32, (COLS, CZ), 1)

    small = [(bnd, bbuf), (lab, labv), (cell, cells), (cell, cellv), (slot, slots),
             (scal, sbuf), (diag, dbuf), (right, rightb), (left, leftb), (near, nearb)]
    loads = [pltpu.make_async_copy(s, d, load_sem.at[i]) for i, (s, d) in enumerate(small)]
    (l_bnd, l_lab, l_cells, l_cellv, l_slot, l_scal, l_diag, l_right, l_left, l_near) = loads
    for l in (l_bnd, l_lab, l_scal):
        l.start()
    for c in range(COLS):
        pltpu.make_async_copy(vol.at[c], vbuf.at[:, c, :], vol_sem).start()
    for l in (l_cells, l_cellv, l_slot, l_right, l_left, l_near, l_diag):
        l.start()

    zero = jnp.zeros((COLS, CZ), F32)
    for x in (0, CX + 1):
        wbuf[x] = jnp.zeros((CY + 2, COLS, CZ), F32)
    for y in (0, CY + 1):
        wbuf[:, y] = jnp.zeros((CX + 2, COLS, CZ), F32)
    zlo[...] = jnp.zeros_like(zlo)
    zhi[...] = jnp.zeros_like(zhi)
    zsend[...] = jnp.zeros_like(zsend)

    barrier = pltpu.get_barrier_semaphore()
    own_group = group == gz

    def greet(device):
        pl.semaphore_signal(barrier, inc=1, device_id=device, device_id_type=MESH)

    for p in range(GROUP):
        source = (gz // 2, lax.rem(gz, 2) * 2 + p // NZ, p % NZ)
        pl.when(jnp.logical_not(jnp.logical_and(own_group, pos == p)))(functools.partial(greet, source))
    for d in range(1, NZ):
        greet((gx, gy, lax.rem(gz + d, NZ)))
    for e in range(1, PEERS):
        other = lax.rem(me2 + e, PEERS)
        greet((other // NY, lax.rem(other, NY), gz))
    own = own_group.astype(jnp.int32)

    l_bnd.wait()
    l_lab.wait()
    pl.semaphore_wait(barrier, GROUP - own + (NZ - 1) + (PEERS - 1))

    def x_copy(t):
        return pltpu.make_async_remote_copy(
            bbuf, xbuf.at[pos], xs_sem.at[t], xr_sem,
            device_id=(t // NY, t % NY, group), device_id_type=MESH)

    x_self = pltpu.make_async_copy(bbuf, xbuf.at[pos], xr_sem)
    for t in range(GROUP):
        mine = jnp.logical_and(own_group, me2 == t)
        pl.when(jnp.logical_not(mine))(lambda t=t: x_copy(t).start())
    pl.when(own_group)(lambda: x_self.start())
    lbuf[gz] = labv[...]
    label_sends = [
        pltpu.make_async_remote_copy(
            labv, lbuf.at[gz], ls_sem, lr_sem,
            device_id=(gx, gy, lax.rem(gz + d, NZ)), device_id_type=MESH)
        for d in range(1, NZ)]
    for s in label_sends:
        s.start()

    l_scal.wait()
    pltpu.make_async_copy(vbuf, vbuf, vol_sem).wait()

    scale_pass(sbuf, vbuf, wbuf)

    halo = []
    for i, (dx, dy) in enumerate(NEIGHBOURS):
        (fx, tx), (fy, ty) = face(dx, CX), face(dy, CY)
        copy = pltpu.make_async_remote_copy(
            wbuf.at[fx, fy], wbuf.at[tx, ty], hs_sem.at[i], hr_sem.at[i],
            device_id=(lax.rem(gx + dx + NX, NX), lax.rem(gy + dy + NY, NY), gz), device_id_type=MESH)

        def within(a, b):
            return jnp.logical_and(jnp.logical_and(a >= 0, a < NX), jnp.logical_and(b >= 0, b < NY))

        to, come = within(gx + dx, gy + dy), within(gx - dx, gy - dy)
        pl.when(to)(copy.start)
        halo.append((copy, to, come))

    l_cells.wait()
    l_cellv.wait()

    trbuf[...] = trace_nodes(cells, vbuf, lane)
    line_weights(wz, ez)
    node_columns(cellv, ohz)
    l_diag.wait()
    node_pass(bbuf, cellv, ohz, vbuf, dbuf, lhs, obuf)

    l_slot.wait()
    l_right.wait()
    l_left.wait()
    l_near.wait()
    pltpu.make_async_copy(xbuf, xbuf, xr_sem).wait()
    tile_products(xbuf, slots, rightb, leftb, nearb, pbuf)
    pltpu.make_async_copy(lbuf.at[pl.ds(0, NZ - 1)], lbuf.at[pl.ds(0, NZ - 1)], lr_sem).wait()
    conductor_sums(trbuf, labv, lbuf, pbuf, mbuf)

    row_sends = []
    for d in range(1, NZ):
        other = lax.rem(gz + d, NZ)
        row_sends.append(pltpu.make_async_remote_copy(
            mbuf.at[other], rbuf.at[gz], ms_sem, mr_sem,
            device_id=(gx, gy, other), device_id_type=MESH))
    for s in row_sends:
        s.start()
    rbuf[gz] = mbuf[gz]

    for copy, to, come in halo:
        pl.when(come)(copy.wait_recv)

    line_pass(wbuf, lhs, qbuf)
    sum_pass(lhs, wz, qbuf, sbuf, obuf, zsend, lane)

    up, down = gz + 1 < NZ, gz > 0
    z_up = pltpu.make_async_remote_copy(
        zsend, zlo, zs_sem.at[0], zr_sem.at[0],
        device_id=(gx, gy, lax.rem(gz + 1, NZ)), device_id_type=MESH)
    z_down = pltpu.make_async_remote_copy(
        zsend, zhi, zs_sem.at[1], zr_sem.at[1],
        device_id=(gx, gy, lax.rem(gz + NZ - 1, NZ)), device_id_type=MESH)
    pl.when(up)(z_up.start)
    pl.when(down)(z_down.start)

    pltpu.make_async_copy(rbuf.at[pl.ds(0, NZ - 1)], rbuf.at[pl.ds(0, NZ - 1)], mr_sem).wait()
    total = rbuf[0]
    for b in range(1, NZ):
        total = total + rbuf[b]
    bnd_out[...] = trbuf[...] + total[:COLS]
    c1[...] = total[COLS:]
    c_sends = []
    for e in range(1, PEERS):
        other = lax.rem(me2 + e, PEERS)
        c_sends.append(pltpu.make_async_remote_copy(
            c1, c2.at[me2], cs_sem, cr_sem,
            device_id=(other // NY, lax.rem(other, NY), gz), device_id_type=MESH))
    for s in c_sends:
        s.start()
    c2[me2] = c1[...]

    pl.when(down)(z_up.wait_recv)
    pl.when(up)(z_down.wait_recv)
    end_rows(zlo, zhi, zc, lane)
    end_pass(0, CX, zc, ez, sbuf, obuf)

    pltpu.make_async_copy(c2.at[pl.ds(0, PEERS - 1)], c2.at[pl.ds(0, PEERS - 1)], cr_sem).wait()
    total = c2[0]
    for b in range(1, PEERS):
        total = total + c2[b]
    charges[...] = total[:, :CONDUCTORS] * (CONDUCTORS / (BND * NX * NY * NZ)) ** 0.5

    for t in range(GROUP):
        mine = jnp.logical_and(own_group, me2 == t)
        pl.when(jnp.logical_not(mine))(lambda t=t: x_copy(t).wait_send())
    for s in label_sends + row_sends + c_sends:
        s.wait_send()
    for copy, to, come in halo:
        pl.when(to)(copy.wait_send)
    pl.when(up)(z_up.wait_send)
    pl.when(down)(z_down.wait_send)


def deliver(field, rows, sums, out, bnd_out, charges, sem, small_sem):
    copies = [pltpu.make_async_copy(field.at[:, c, :], out.at[c], sem) for c in range(COLS)]
    copies.append(pltpu.make_async_copy(rows, bnd_out, small_sem.at[0]))
    copies.append(pltpu.make_async_copy(sums, charges, small_sem.at[1]))
    for c in copies:
        c.start()
    pltpu.make_async_copy(field, field, sem).wait()
    copies[-2].wait()
    copies[-1].wait()


def shards(vol, scal, diag, bnd, cell, lab, left, right, near, slot):
    nodes = CX * CY
    field = (nodes, COLS, CZ)
    dma = pltpu.SemaphoreType.DMA
    hbm_spec = pl.BlockSpec(memory_space=pltpu.HBM)
    vmem_spec = pl.BlockSpec(memory_space=pltpu.VMEM)
    operands = (
        vol.reshape(COLS, nodes, CZ), scal, diag, bnd, cell.reshape(1, BND), lab.reshape(1, BND),
        left.reshape(ROWS, TB, TB), right.reshape(ROWS, TB, TB), near.reshape(ROWS, TB, TB), slot,
    )
    operands = [pltpu.with_memory_space_constraint(o, pltpu.HBM) for o in operands]
    results = pl.pallas_call(
        kernel,
        out_shape=(
            pltpu.VMEM(field, F32),
            pltpu.VMEM((COLS, BND), F32),
            pltpu.VMEM((COLS, CONDUCTORS), F32),
        ),
        in_specs=[hbm_spec] * len(operands),
        out_specs=(vmem_spec,) * 3,
        scratch_shapes=[
            pltpu.VMEM(field, F32),
            pltpu.VMEM((CX + 2, CY + 2, COLS, CZ), F32),
            pltpu.VMEM(field, F32),
            pltpu.VMEM((CX, CY * COLS, 2 * CZ), BF16),
            pltpu.VMEM((CX, CY, CZ), F32),
            pltpu.VMEM((CX, CY, CZ), F32),
            pltpu.VMEM((COLS, BND), F32),
            pltpu.VMEM((1, BND), jnp.int32),
            pltpu.SMEM((1, BND), jnp.int32),
            pltpu.VMEM((1, BND), jnp.int32),
            pltpu.SMEM((ROWS, TILES), jnp.int32),
            pltpu.VMEM((ROWS, TB, TB), BF16),
            pltpu.VMEM((ROWS, TB, TB), BF16),
            pltpu.VMEM((ROWS, TB, TB), BF16),
            pltpu.VMEM((GROUP, COLS, BND), F32),
            pltpu.VMEM((NZ, 1, BND), jnp.int32),
            pltpu.VMEM((CZ, 2 * BND), BF16),
            pltpu.VMEM((2 * CZ, 2 * CZ), BF16),
            pltpu.VMEM((2 * CZ, CZ), BF16),
            pltpu.VMEM((CY * COLS, 2 * CZ), BF16),
            pltpu.VMEM((NZ, COLS, BND), F32),
            pltpu.VMEM((NZ, 2 * COLS, BND), F32),
            pltpu.VMEM((NZ, 2 * COLS, BND), F32),
            pltpu.VMEM((COLS, BND), F32),
            pltpu.VMEM((PEERS, COLS, BND), F32),
            pltpu.VMEM((CY // 2, COLS, CZ), F32),
            pltpu.VMEM((CY // 2, COLS, CZ), F32),
            pltpu.VMEM((CY // 2, COLS, CZ), F32),
            pltpu.VMEM((COLS, BND), F32),
            dma((10,)), dma, dma((GROUP,)), dma, dma, dma, dma((8,)), dma((8,)),
            dma, dma, dma((2,)), dma((2,)), dma, dma,
        ],
        compiler_params=pltpu.CompilerParams(
            collective_id=0, has_side_effects=True, vmem_limit_bytes=40 * 1024 * 1024),
    )(*operands)
    out, bnd_out, charges = pl.pallas_call(
        deliver,
        out_shape=(
            pltpu.HBM((COLS, nodes, CZ), F32),
            pltpu.HBM((COLS, BND), F32),
            pltpu.HBM((COLS, CONDUCTORS), F32),
        ),
        in_specs=[vmem_spec] * 3,
        out_specs=(hbm_spec,) * 3,
        scratch_shapes=[dma, dma((2,))],
    )(*[pltpu.with_memory_space_constraint(r, pltpu.VMEM) for r in results])
    return out.reshape(vol.shape), bnd_out, charges.T


def solution(mesh):
    in_specs = (
        P(None, "gx", "gy", "gz"),
        P("gx", "gy", "gz"),
        P("gx", "gy", "gz"),
        P(None, ("gx", "gy", "gz")),
        P(("gx", "gy", "gz")),
        P(("gx", "gy", "gz")),
        P(("gx", "gy"), "gz", None, None),
        P(("gx", "gy"), "gz", None, None),
        P(("gx", "gy"), "gz", None, None),
        P(("gx", "gy"), "gz"),
    )
    out_specs = (P(None, "gx", "gy", "gz"), P(None, ("gx", "gy", "gz")), P())
    return jax.shard_map(shards, mesh=mesh, in_specs=in_specs, out_specs=out_specs, check_vma=False)
```

```python
import functools

import jax
import jax.numpy as jnp
from jax import lax
from jax.experimental import pallas as pl
from jax.experimental.pallas import tpu as pltpu
from jax.sharding import PartitionSpec as P

MESH = pl.DeviceIdType.MESH
F32 = jnp.float32
BF16 = jnp.bfloat16

NX, NY, NZ = 4, 4, 8
PEERS = NX * NY
COLS, CX, CY, CZ = 8, 32, 16, 128
ROWS, TILES, RANK, TB = 4, 8, 32, 256
CONDUCTORS = 32
BND = 128
GROUP = PEERS
PLANE = [(3, 2), (2, 2), (3, 1), (3, 3), (2, 1), (2, 3), (1, 2), (0, 2), (3, 0), (2, 0), (1, 1), (1, 3), (0, 1), (0, 3), (1, 0)]
LINE = [5, 4, 7, 3, 6, 2, 1]
FIRST = [(3, 0), (2, 0), (3, 1), (2, 1), (1, 1), (0, 1), (1, 0)]
SECOND = [(2, 2), (2, 1), (2, 3), (1, 2), (3, 2), (2, 0), (0, 2), (1, 1), (1, 3), (3, 1), (3, 3), (1, 0), (3, 0), (0, 1), (0, 3)]
NEIGHBOURS = [(dx, dy) for dx in (-1, 0, 1) for dy in (-1, 0, 1) if (dx, dy) != (0, 0)]


def split(x):
    hi = x.astype(BF16).astype(F32)
    return hi, x - hi


def stacked(x):
    hi, lo = split(x)
    return jnp.concatenate([hi, lo], axis=0).astype(BF16)


def dot(a, b):
    return lax.dot_general(a, b, (((1,), (0,)), ((), ())), preferred_element_type=F32)


def dot_nt(a, b):
    return lax.dot_general(a, b, (((1,), (1,)), ((), ())), preferred_element_type=F32)


def total_of(buf):
    parts = [buf[i] for i in range(buf.shape[0])]
    while len(parts) > 1:
        parts = [a + b for a, b in zip(parts[::2], parts[1::2])]
    return parts[0]


def face(step, size):
    if step == 0:
        return pl.ds(1, size), pl.ds(1, size)
    return (pl.ds(size, 1), pl.ds(0, 1)) if step > 0 else (pl.ds(1, 1), pl.ds(size + 1, 1))


GX = 8


def scale_pass(sbuf, vbuf, wbuf):
    @pl.loop(0, CX)
    def _(x):
        for y in range(CY):
            s = sbuf[x, pl.ds(y, 1), :] * (1.0 / 6.0)
            wbuf[x + 1, y + 1] = jnp.broadcast_to(s, (COLS, CZ)) * vbuf[x * CY + y]


def line_weights(wz, ez):
    z = lax.broadcasted_iota(jnp.int32, (CZ, CZ), 0)
    n = lax.broadcasted_iota(jnp.int32, (CZ, CZ), 1)
    near = jnp.logical_or(z == n + 1, z == n - 1)
    first = jnp.bitwise_and(n, CX) == 0
    ends = jnp.logical_or(jnp.logical_and(z == 0, first), jnp.logical_and(z == CZ - 1, jnp.logical_not(first)))
    from_above = jnp.bitwise_and(z, CX) == 0
    land = jnp.logical_or(jnp.logical_and(n == CZ - 1, from_above), jnp.logical_and(n == 0, jnp.logical_not(from_above)))

    def ones(mask):
        return mask.astype(F32).astype(BF16)

    for piece in range(2):
        rows = pl.ds(piece * CZ, CZ)
        wz[rows, pl.ds(0, CZ)] = ones(near)
        wz[rows, pl.ds(CZ, CZ)] = ones(ends)
        ez[rows, :] = ones(land)


def node_columns(cellv, ohz):
    zk = jnp.bitwise_and(cellv[...], CZ - 1)
    onehot = (lax.broadcasted_iota(jnp.int32, (CZ, BND), 0) == zk).astype(F32).astype(BF16)
    ohz[:, pl.ds(0, BND)] = onehot
    ohz[:, pl.ds(BND, BND)] = onehot


def node_pass(bbuf, cellv, ohz, vbuf, dbuf, lhs, obuf):
    spots = jnp.broadcast_to(lax.shift_right_logical(cellv[...], 7), (COLS, BND))
    pieces = split(bbuf[...])

    @pl.loop(0, CX)
    def _(x):
        for y in range(0, CY, 2):
            here = [spots == x * CY + y, spots == x * CY + y + 1]
            for p in range(2):
                both = jnp.concatenate([jnp.where(h, pieces[p], 0.0) for h in here], axis=0)
                lhs[x, pl.ds(COLS * y, 2 * COLS), pl.ds(p * BND, BND)] = both.astype(BF16)

    @pl.loop(0, CX // GX)
    def _(g):
        extra = dot_nt(lhs[pl.ds(g * GX, GX)].reshape(GX * CY * COLS, 2 * BND), ohz[...])
        for i in range(GX):
            for y in range(CY):
                x = g * GX + i
                d = jnp.broadcast_to(dbuf[x, pl.ds(y, 1), :], (COLS, CZ))
                k = (i * CY + y) * COLS
                obuf[x * CY + y] = d * vbuf[x * CY + y] + extra[k:k + COLS]


def line_pass(wbuf, lhs, qbuf):
    @pl.loop(0, CX)
    def _(x):
        a = [wbuf[x, y] + wbuf[x + 2, y] for y in range(CY + 2)]
        w = [wbuf[x + 1, y] for y in range(CY + 2)]
        for y0 in range(0, CY, 2):
            ts = []
            for y in (y0, y0 + 1):
                p = a[y] + a[y + 2]
                ts.append((a[y + 1] + (w[y] + w[y + 2])) + 0.5 * p)
                qbuf[x * CY + y] = 16.0 * w[y + 1] - p
            t = jnp.concatenate(ts, axis=0)
            hi = t.astype(BF16)
            lhs[x, pl.ds(COLS * y0, 2 * COLS), pl.ds(0, CZ)] = hi
            lhs[x, pl.ds(COLS * y0, 2 * COLS), pl.ds(CZ, CZ)] = (t - hi.astype(F32)).astype(BF16)


def sum_pass(lhs, wz, qbuf, sbuf, obuf, zsend, lane):
    spot = jnp.bitwise_and(lane, CX - 1)
    half = lax.shift_right_logical(lane, 6)

    @pl.loop(0, CX // GX)
    def _(g):
        r = dot(lhs[pl.ds(g * GX, GX)].reshape(GX * CY * COLS, 2 * CZ), wz[...])
        ends = [zsend[y] for y in range(CY // 2)]
        for i in range(GX):
            x = g * GX + i
            mine = [jnp.logical_and(half == h, spot == x) for h in range(2)]
            for y in range(CY):
                k = (i * CY + y) * COLS
                s = jnp.broadcast_to(sbuf[x, pl.ds(y, 1), :], (COLS, CZ))
                obuf[x * CY + y] = obuf[x * CY + y] + s * (qbuf[x * CY + y] - r[k:k + COLS, :CZ])
                e = y % (CY // 2)
                ends[e] = jnp.where(mine[y // (CY // 2)], r[k:k + COLS, CZ:], ends[e])
        for y in range(CY // 2):
            zsend[y] = ends[y]


def end_rows(zlo, zhi, zc, lane):
    above = jnp.bitwise_and(lane, CX) == 0
    for y in range(0, CY, 2):
        e = y % (CY // 2)
        both = []
        for k in (e, e + 1):
            row = jnp.where(above, zhi[k], zlo[k])
            both.append(jnp.where(lax.shift_right_logical(lane, 6) == y // (CY // 2), row, 0.0))
        z = jnp.concatenate(both, axis=0)
        hi = z.astype(BF16)
        zc[pl.ds(COLS * y, 2 * COLS), pl.ds(0, CZ)] = hi
        zc[pl.ds(COLS * y, 2 * COLS), pl.ds(CZ, CZ)] = (z - hi.astype(F32)).astype(BF16)


def end_pass(k, chunk, zc, ez, sbuf, obuf):
    lane2 = jnp.bitwise_and(lax.broadcasted_iota(jnp.int32, (2 * COLS, 2 * CZ), 1), CX - 1)

    @pl.loop(k * (chunk // GX), (k + 1) * (chunk // GX))
    def _(g):
        rows = []
        for i in range(GX):
            here = (lane2 == g * GX + i).astype(F32).astype(BF16)
            for y in range(0, CY, 2):
                rows.append(zc[pl.ds(COLS * y, 2 * COLS), :] * here)
        h = dot(jnp.concatenate(rows, axis=0), ez[...])
        for i in range(GX):
            x = g * GX + i
            for y in range(CY):
                q = (i * CY + y) * COLS
                s = jnp.broadcast_to(sbuf[x, pl.ds(y, 1), :], (COLS, CZ))
                obuf[x * CY + y] = obuf[x * CY + y] - s * h[q:q + COLS]


def trace_nodes(cells, vbuf, lane):
    def trace_one(k, acc):
        place = cells[0, k]
        row = vbuf[lax.shift_right_logical(place, 7)]
        turn = jnp.bitwise_and(k + CZ - jnp.bitwise_and(place, CZ - 1), CZ - 1)
        return jnp.where(lane == k, pltpu.roll(row, turn, 1), acc)

    return lax.fori_loop(0, BND, trace_one, jnp.zeros((COLS, CZ), F32), unroll=8)


def tile_products(xbuf, slots, rightb, leftb, nearb):
    pieces = []
    for j in range(TILES):
        xj = jnp.concatenate([xbuf[2 * j], xbuf[2 * j + 1]], axis=1)
        hi, lo = split(xj)
        pieces.append(jnp.concatenate([hi, lo], axis=0))
    xall = jnp.concatenate(pieces, axis=0).astype(BF16)
    lane2 = lax.broadcasted_iota(jnp.int32, (COLS, TB), 1)
    parts = []
    for i in range(ROWS):
        proj = dot_nt(xall, rightb[i])
        acc = jnp.zeros((COLS, TB), F32)
        chosen = jnp.zeros((2 * COLS, TB), F32)
        for j in range(TILES):
            far = jnp.where(slots[i, j] < 0, 1.0, 0.0).astype(F32)
            block = proj[16 * j:16 * j + 8] + proj[16 * j + 8:16 * j + 16]
            acc = jnp.where(lane2 // RANK == j, block * far, acc)
            chosen = chosen + pieces[j] * (1.0 - far)
        both = dot(stacked(acc), leftb[i]) + dot_nt(chosen.astype(BF16), nearb[i])
        parts.append(-(both[:COLS] + both[COLS:]))
    return jnp.concatenate(parts, axis=1)


def members(labels):
    which = lax.broadcasted_iota(jnp.int32, (CONDUCTORS, BND), 0)
    return (which == labels).astype(F32).astype(BF16)


def conductor_sums(values, onehots):
    both = dot_nt(stacked(values), onehots)
    return both[:COLS] + both[COLS:]


def kernel(
    vol, scal, diag, bnd, cell, lab, left, right, near, slot,
    obuf, bnd_out, charges,
    vbuf, wbuf, qbuf, lhs, sbuf, dbuf, bbuf, cellv, cells, labv, slots, leftb, rightb, nearb,
    xbuf, lbuf, memb, ohz, wz, ez, zc, pbuf, rbuf, c1, c2, c3, c4, zsend, zlo, zhi, trbuf,
    load_sem, vol_sem, xs_sem, xr_sem, ls_sem, lr_sem, hs_sem, hr_sem,
    ms_sem, mr_sem, zs_sem, zr_sem, cs_sem, cr_sem, ds_sem, dr_sem,
):
    gx, gy, gz = lax.axis_index("gx"), lax.axis_index("gy"), lax.axis_index("gz")
    group = (gx * NY + gy) // 2
    pos = lax.rem(gy, 2) * NZ + gz
    own_group = group == gz
    lane = lax.broadcasted_iota(jnp.int32, (COLS, CZ), 1)

    def remote(src, dst, send_sem, recv_sem, device):
        return pltpu.make_async_remote_copy(src, dst, send_sem, recv_sem, device_id=device, device_id_type=MESH)

    def plane(a, b):
        return jnp.bitwise_xor(gx, a), lax.rem(gy + b, NY)

    def line(k):
        return gx, gy, jnp.bitwise_xor(gz, k)

    first = [(jnp.bitwise_xor(gx, a), gy, jnp.bitwise_xor(gz, b)) for a, b in FIRST]
    second = [(jnp.bitwise_xor(gx, 1), lax.rem(gy + b, NY), jnp.bitwise_xor(gz, 2 * c)) for b, c in SECOND]

    small = [(bnd, bbuf), (lab, labv), (cell, cells), (cell, cellv), (slot, slots),
             (scal, sbuf), (diag, dbuf), (right, rightb), (left, leftb), (near, nearb)]
    loads = [pltpu.make_async_copy(s, d, load_sem.at[i]) for i, (s, d) in enumerate(small)]
    (l_bnd, l_lab, l_cells, l_cellv, l_slot, l_scal, l_diag, l_right, l_left, l_near) = loads
    l_bnd.start()
    l_lab.start()

    for x in (0, CX + 1):
        wbuf[x] = jnp.zeros((CY + 2, COLS, CZ), F32)
    for y in (0, CY + 1):
        wbuf[:, y] = jnp.zeros((CX + 2, COLS, CZ), F32)
    zlo[...] = jnp.zeros_like(zlo)
    zhi[...] = jnp.zeros_like(zhi)

    barrier = pltpu.get_barrier_semaphore()

    def greet(device):
        pl.semaphore_signal(barrier, inc=1, device_id=device, device_id_type=MESH)

    for k in LINE + [0]:
        for p in range(2):
            source = (gz // 2, lax.rem(gz, 2) * 2 + p, jnp.bitwise_xor(gz, k))
            if k:
                greet(source)
            else:
                here = jnp.logical_and(own_group, lax.rem(gy, 2) == p)
                pl.when(jnp.logical_not(here))(functools.partial(greet, source))
    for device in second:
        greet(device)
    for k in LINE:
        greet(line(k))
    for device in first:
        greet(device)

    def within(a, b):
        return jnp.logical_and(jnp.logical_and(a >= 0, a < NX), jnp.logical_and(b >= 0, b < NY))

    halo = []
    count = GROUP - own_group.astype(jnp.int32) + len(SECOND) + len(LINE) + len(FIRST)
    for i, (dx, dy) in enumerate(NEIGHBOURS):
        (fx, tx), (fy, ty) = face(dx, CX), face(dy, CY)
        device = (lax.rem(gx + dx + NX, NX), lax.rem(gy + dy + NY, NY), gz)
        to, come = within(gx + dx, gy + dy), within(gx - dx, gy - dy)
        halo.append((remote(wbuf.at[fx, fy], wbuf.at[tx, ty], hs_sem.at[i], hr_sem.at[i], device), to, come))
        pl.when(to)(functools.partial(greet, device))
        count = count + come.astype(jnp.int32)

    l_scal.start()
    for c in range(COLS):
        pltpu.make_async_copy(vol.at[c], vbuf.at[:, c, :], vol_sem).start()
    for l in (l_cells, l_cellv, l_diag, l_slot, l_right, l_left, l_near):
        l.start()
    l_bnd.wait()
    l_lab.wait()
    pl.semaphore_wait(barrier, count)

    x_sends = [remote(bbuf, xbuf.at[pos], xs_sem.at[i], xr_sem, (*plane(a, b), group)) for i, (a, b) in enumerate(PLANE)]
    x_last = remote(bbuf, xbuf.at[pos], xs_sem.at[len(PLANE)], xr_sem, (gx, gy, group))
    x_self = pltpu.make_async_copy(bbuf, xbuf.at[pos], xr_sem)
    for s in x_sends:
        s.start()
    pl.when(jnp.logical_not(own_group))(x_last.start)
    pl.when(own_group)(x_self.start)
    label_sends = [remote(labv, lbuf.at[gz], ls_sem, lr_sem, line(k)) for k in LINE]
    for s in label_sends:
        s.start()
    lbuf[gz] = labv[...]

    l_scal.wait()
    pltpu.make_async_copy(vbuf, vbuf, vol_sem).wait()
    scale_pass(sbuf, vbuf, wbuf)
    for copy, to, come in halo:
        pl.when(to)(copy.start)

    l_cells.wait()
    l_cellv.wait()
    l_diag.wait()
    trbuf[...] = trace_nodes(cells, vbuf, lane)
    line_weights(wz, ez)
    node_columns(cellv, ohz)
    node_pass(bbuf, cellv, ohz, vbuf, dbuf, lhs, obuf)
    zsend[...] = jnp.zeros_like(zsend)
    c1[...] = jnp.zeros_like(c1)
    own_sums = conductor_sums(trbuf[...], members(labv[...]))

    pltpu.make_async_copy(lbuf.at[pl.ds(0, NZ - 1)], lbuf.at[pl.ds(0, NZ - 1)], lr_sem).wait()
    for b in range(NZ):
        memb[:, pl.ds(b * BND, BND)] = members(lbuf[b])

    l_slot.wait()
    l_right.wait()
    l_left.wait()
    l_near.wait()
    pltpu.make_async_copy(xbuf, xbuf, xr_sem).wait()
    values = tile_products(xbuf, slots, rightb, leftb, nearb)
    c1[:, pl.ds(0, CONDUCTORS)] = own_sums + conductor_sums(values, memb[...])
    place = gx * 2 + lax.rem(gz, 2)
    first_sends = [remote(c1, c2.at[place], cs_sem, cr_sem, device) for device in first]
    for s in first_sends:
        s.start()
    c2[place] = c1[...]

    for b in range(NZ):
        pbuf[b] = values[:, b * BND:(b + 1) * BND]
    row_sends = [remote(pbuf.at[jnp.bitwise_xor(gz, k)], rbuf.at[gz], ms_sem, mr_sem, line(k)) for k in LINE]
    for s in row_sends:
        s.start()
    rbuf[gz] = pbuf[gz]

    for copy, to, come in halo:
        pl.when(come)(copy.wait_recv)
    line_pass(wbuf, lhs, qbuf)
    sum_pass(lhs, wz, qbuf, sbuf, obuf, zsend, lane)
    up, down = gz + 1 < NZ, gz > 0
    z_up = remote(zsend, zlo, zs_sem.at[0], zr_sem.at[0], (gx, gy, lax.rem(gz + 1, NZ)))
    z_down = remote(zsend, zhi, zs_sem.at[1], zr_sem.at[1], (gx, gy, lax.rem(gz + NZ - 1, NZ)))
    pl.when(up)(z_up.start)
    pl.when(down)(z_down.start)

    pltpu.make_async_copy(c2.at[pl.ds(0, len(FIRST))], c2.at[pl.ds(0, len(FIRST))], cr_sem).wait()
    c3[...] = total_of(c2)
    place = gy * 4 + gz // 2
    second_sends = [remote(c3, c4.at[place], ds_sem, dr_sem, device) for device in second]
    for s in second_sends:
        s.start()
    c4[place] = c3[...]

    pltpu.make_async_copy(rbuf.at[pl.ds(0, NZ - 1)], rbuf.at[pl.ds(0, NZ - 1)], mr_sem).wait()
    bnd_out[...] = trbuf[...] + total_of(rbuf)
    pl.when(down)(z_up.wait_recv)
    pl.when(up)(z_down.wait_recv)
    end_rows(zlo, zhi, zc, lane)
    end_pass(0, CX, zc, ez, sbuf, obuf)

    for s in x_sends + label_sends + first_sends + row_sends + second_sends:
        s.wait_send()
    pl.when(jnp.logical_not(own_group))(x_last.wait_send)
    for copy, to, come in halo:
        pl.when(to)(copy.wait_send)
    pl.when(up)(z_up.wait_send)
    pl.when(down)(z_down.wait_send)

    pltpu.make_async_copy(c4.at[pl.ds(0, len(SECOND))], c4.at[pl.ds(0, len(SECOND))], dr_sem).wait()
    charges[...] = total_of(c4)[:, :CONDUCTORS] * (CONDUCTORS / (BND * NX * NY * NZ)) ** 0.5


def deliver(field, rows, sums, out, bnd_out, charges, sem, small_sem):
    copies = [pltpu.make_async_copy(field.at[:, c, :], out.at[c], sem) for c in range(COLS)]
    copies.append(pltpu.make_async_copy(rows, bnd_out, small_sem.at[0]))
    copies.append(pltpu.make_async_copy(sums, charges, small_sem.at[1]))
    for c in copies:
        c.start()
    pltpu.make_async_copy(field, field, sem).wait()
    copies[-2].wait()
    copies[-1].wait()


def shards(vol, scal, diag, bnd, cell, lab, left, right, near, slot):
    nodes = CX * CY
    field = (nodes, COLS, CZ)
    dma = pltpu.SemaphoreType.DMA
    hbm_spec = pl.BlockSpec(memory_space=pltpu.HBM)
    vmem_spec = pl.BlockSpec(memory_space=pltpu.VMEM)
    operands = (
        vol.reshape(COLS, nodes, CZ), scal, diag, bnd, cell.reshape(1, BND), lab.reshape(1, BND),
        left.reshape(ROWS, TB, TB), right.reshape(ROWS, TB, TB), near.reshape(ROWS, TB, TB), slot,
    )
    operands = [pltpu.with_memory_space_constraint(o, pltpu.HBM) for o in operands]
    results = pl.pallas_call(
        kernel,
        out_shape=(
            pltpu.VMEM(field, F32),
            pltpu.VMEM((COLS, BND), F32),
            pltpu.VMEM((COLS, CONDUCTORS), F32),
        ),
        in_specs=[hbm_spec] * len(operands),
        out_specs=(vmem_spec,) * 3,
        scratch_shapes=[
            pltpu.VMEM(field, F32),
            pltpu.VMEM((CX + 2, CY + 2, COLS, CZ), F32),
            pltpu.VMEM(field, F32),
            pltpu.VMEM((CX, CY * COLS, 2 * CZ), BF16),
            pltpu.VMEM((CX, CY, CZ), F32),
            pltpu.VMEM((CX, CY, CZ), F32),
            pltpu.VMEM((COLS, BND), F32),
            pltpu.VMEM((1, BND), jnp.int32),
            pltpu.SMEM((1, BND), jnp.int32),
            pltpu.VMEM((1, BND), jnp.int32),
            pltpu.SMEM((ROWS, TILES), jnp.int32),
            pltpu.VMEM((ROWS, TB, TB), BF16),
            pltpu.VMEM((ROWS, TB, TB), BF16),
            pltpu.VMEM((ROWS, TB, TB), BF16),
            pltpu.VMEM((GROUP, COLS, BND), F32),
            pltpu.VMEM((NZ, 1, BND), jnp.int32),
            pltpu.VMEM((CONDUCTORS, NZ * BND), BF16),
            pltpu.VMEM((CZ, 2 * BND), BF16),
            pltpu.VMEM((2 * CZ, 2 * CZ), BF16),
            pltpu.VMEM((2 * CZ, CZ), BF16),
            pltpu.VMEM((CY * COLS, 2 * CZ), BF16),
            pltpu.VMEM((NZ, COLS, BND), F32),
            pltpu.VMEM((NZ, COLS, BND), F32),
            pltpu.VMEM((COLS, BND), F32),
            pltpu.VMEM((len(FIRST) + 1, COLS, BND), F32),
            pltpu.VMEM((COLS, BND), F32),
            pltpu.VMEM((len(SECOND) + 1, COLS, BND), F32),
            pltpu.VMEM((CY // 2, COLS, CZ), F32),
            pltpu.VMEM((CY // 2, COLS, CZ), F32),
            pltpu.VMEM((CY // 2, COLS, CZ), F32),
            pltpu.VMEM((COLS, BND), F32),
            dma((10,)), dma, dma((GROUP,)), dma, dma, dma, dma((8,)), dma((8,)),
            dma, dma, dma((2,)), dma((2,)), dma, dma, dma, dma,
        ],
        compiler_params=pltpu.CompilerParams(
            collective_id=0, has_side_effects=True, vmem_limit_bytes=40 * 1024 * 1024),
    )(*operands)
    out, bnd_out, charges = pl.pallas_call(
        deliver,
        out_shape=(
            pltpu.HBM((COLS, nodes, CZ), F32),
            pltpu.HBM((COLS, BND), F32),
            pltpu.HBM((COLS, CONDUCTORS), F32),
        ),
        in_specs=[vmem_spec] * 3,
        out_specs=(hbm_spec,) * 3,
        scratch_shapes=[dma, dma((2,))],
    )(*[pltpu.with_memory_space_constraint(r, pltpu.VMEM) for r in results])
    return out.reshape(vol.shape), bnd_out, charges.T


def solution(mesh):
    in_specs = (
        P(None, "gx", "gy", "gz"),
        P("gx", "gy", "gz"),
        P("gx", "gy", "gz"),
        P(None, ("gx", "gy", "gz")),
        P(("gx", "gy", "gz")),
        P(("gx", "gy", "gz")),
        P(("gx", "gy"), "gz", None, None),
        P(("gx", "gy"), "gz", None, None),
        P(("gx", "gy"), "gz", None, None),
        P(("gx", "gy"), "gz"),
    )
    out_specs = (P(None, "gx", "gy", "gz"), P(None, ("gx", "gy", "gz")), P())
    return jax.shard_map(shards, mesh=mesh, in_specs=in_specs, out_specs=out_specs, check_vma=False)
```

```python
import functools

import jax
import jax.numpy as jnp
from jax import lax
from jax.experimental import pallas as pl
from jax.experimental.pallas import tpu as pltpu
from jax.sharding import PartitionSpec as P

MESH = pl.DeviceIdType.MESH
F32 = jnp.float32
BF16 = jnp.bfloat16

NX, NY, NZ = 4, 4, 8
PEERS = NX * NY
COLS, CX, CY, CZ = 8, 32, 16, 128
ROWS, TILES, RANK, TB = 4, 8, 32, 256
CONDUCTORS = 32
BND = 128
GROUP = PEERS
PLANE = [(3, 2), (2, 2), (3, 1), (3, 3), (2, 1), (2, 3), (1, 2), (0, 2), (3, 0), (2, 0), (1, 1), (1, 3), (0, 1), (0, 3), (1, 0)]
LINE = [5, 4, 7, 3, 6, 2, 1]
FIRST = [(3, 0), (2, 0), (3, 1), (2, 1), (1, 1), (0, 1), (1, 0)]
SECOND = [(2, 2), (2, 1), (2, 3), (1, 2), (3, 2), (2, 0), (0, 2), (1, 1), (1, 3), (3, 1), (3, 3), (1, 0), (3, 0), (0, 1), (0, 3)]
HEAD = (1, 0, 0)
NEIGHBOURS = [(dx, dy) for dx in (-1, 0, 1) for dy in (-1, 0, 1) if (dx, dy) != (0, 0)]


def split(x):
    hi = x.astype(BF16).astype(F32)
    return hi, x - hi


def stacked(x):
    hi, lo = split(x)
    return jnp.concatenate([hi, lo], axis=0).astype(BF16)


def dot(a, b):
    return lax.dot_general(a, b, (((1,), (0,)), ((), ())), preferred_element_type=F32)


def dot_nt(a, b):
    return lax.dot_general(a, b, (((1,), (1,)), ((), ())), preferred_element_type=F32)


def total_of(buf):
    parts = [buf[i] for i in range(buf.shape[0])]
    while len(parts) > 1:
        parts = [a + b for a, b in zip(parts[::2], parts[1::2])]
    return parts[0]


def face(step, size):
    if step == 0:
        return pl.ds(1, size), pl.ds(1, size)
    return (pl.ds(size, 1), pl.ds(0, 1)) if step > 0 else (pl.ds(1, 1), pl.ds(size + 1, 1))


GX = 8


def scale_pass(sbuf, vbuf, wbuf):
    @pl.loop(0, CX)
    def _(x):
        for y in range(CY):
            s = sbuf[x, pl.ds(y, 1), :] * (1.0 / 6.0)
            wbuf[x + 1, y + 1] = jnp.broadcast_to(s, (COLS, CZ)) * vbuf[x * CY + y]


def line_weights(wz, ez):
    z = lax.broadcasted_iota(jnp.int32, (CZ, CZ), 0)
    n = lax.broadcasted_iota(jnp.int32, (CZ, CZ), 1)
    near = jnp.logical_or(z == n + 1, z == n - 1)
    first = jnp.bitwise_and(n, CX) == 0
    ends = jnp.logical_or(jnp.logical_and(z == 0, first), jnp.logical_and(z == CZ - 1, jnp.logical_not(first)))
    from_above = jnp.bitwise_and(z, CX) == 0
    land = jnp.logical_or(jnp.logical_and(n == CZ - 1, from_above), jnp.logical_and(n == 0, jnp.logical_not(from_above)))

    def ones(mask):
        return mask.astype(F32).astype(BF16)

    for piece in range(2):
        rows = pl.ds(piece * CZ, CZ)
        wz[rows, pl.ds(0, CZ)] = ones(near)
        wz[rows, pl.ds(CZ, CZ)] = ones(ends)
        ez[rows, :] = ones(land)


def node_columns(cellv, ohz):
    zk = jnp.bitwise_and(cellv[...], CZ - 1)
    onehot = (lax.broadcasted_iota(jnp.int32, (CZ, BND), 0) == zk).astype(F32).astype(BF16)
    ohz[:, pl.ds(0, BND)] = onehot
    ohz[:, pl.ds(BND, BND)] = onehot


def node_pass(bbuf, cellv, ohz, vbuf, dbuf, lhs, obuf):
    spots = jnp.broadcast_to(lax.shift_right_logical(cellv[...], 7), (COLS, BND))
    pieces = split(bbuf[...])

    @pl.loop(0, CX)
    def _(x):
        for y in range(0, CY, 2):
            here = [spots == x * CY + y, spots == x * CY + y + 1]
            for p in range(2):
                both = jnp.concatenate([jnp.where(h, pieces[p], 0.0) for h in here], axis=0)
                lhs[x, pl.ds(COLS * y, 2 * COLS), pl.ds(p * BND, BND)] = both.astype(BF16)

    @pl.loop(0, CX // GX)
    def _(g):
        extra = dot_nt(lhs[pl.ds(g * GX, GX)].reshape(GX * CY * COLS, 2 * BND), ohz[...])
        for i in range(GX):
            for y in range(CY):
                x = g * GX + i
                d = jnp.broadcast_to(dbuf[x, pl.ds(y, 1), :], (COLS, CZ))
                k = (i * CY + y) * COLS
                obuf[x * CY + y] = d * vbuf[x * CY + y] + extra[k:k + COLS]


def line_pass(wbuf, lhs, qbuf):
    @pl.loop(0, CX)
    def _(x):
        a = [wbuf[x, y] + wbuf[x + 2, y] for y in range(CY + 2)]
        w = [wbuf[x + 1, y] for y in range(CY + 2)]
        for y0 in range(0, CY, 2):
            ts = []
            for y in (y0, y0 + 1):
                p = a[y] + a[y + 2]
                ts.append((a[y + 1] + (w[y] + w[y + 2])) + 0.5 * p)
                qbuf[x * CY + y] = 16.0 * w[y + 1] - p
            t = jnp.concatenate(ts, axis=0)
            hi = t.astype(BF16)
            lhs[x, pl.ds(COLS * y0, 2 * COLS), pl.ds(0, CZ)] = hi
            lhs[x, pl.ds(COLS * y0, 2 * COLS), pl.ds(CZ, CZ)] = (t - hi.astype(F32)).astype(BF16)


def sum_pass(lhs, wz, qbuf, sbuf, obuf, zsend, lane):
    spot = jnp.bitwise_and(lane, CX - 1)
    half = lax.shift_right_logical(lane, 6)

    @pl.loop(0, CX // GX)
    def _(g):
        r = dot(lhs[pl.ds(g * GX, GX)].reshape(GX * CY * COLS, 2 * CZ), wz[...])
        ends = [zsend[y] for y in range(CY // 2)]
        for i in range(GX):
            x = g * GX + i
            mine = [jnp.logical_and(half == h, spot == x) for h in range(2)]
            for y in range(CY):
                k = (i * CY + y) * COLS
                s = jnp.broadcast_to(sbuf[x, pl.ds(y, 1), :], (COLS, CZ))
                obuf[x * CY + y] = obuf[x * CY + y] + s * (qbuf[x * CY + y] - r[k:k + COLS, :CZ])
                e = y % (CY // 2)
                ends[e] = jnp.where(mine[y // (CY // 2)], r[k:k + COLS, CZ:], ends[e])
        for y in range(CY // 2):
            zsend[y] = ends[y]


def end_rows(zlo, zhi, zc, lane):
    above = jnp.bitwise_and(lane, CX) == 0
    for y in range(0, CY, 2):
        e = y % (CY // 2)
        both = []
        for k in (e, e + 1):
            row = jnp.where(above, zhi[k], zlo[k])
            both.append(jnp.where(lax.shift_right_logical(lane, 6) == y // (CY // 2), row, 0.0))
        z = jnp.concatenate(both, axis=0)
        hi = z.astype(BF16)
        zc[pl.ds(COLS * y, 2 * COLS), pl.ds(0, CZ)] = hi
        zc[pl.ds(COLS * y, 2 * COLS), pl.ds(CZ, CZ)] = (z - hi.astype(F32)).astype(BF16)


def end_pass(k, chunk, zc, ez, sbuf, obuf):
    lane2 = jnp.bitwise_and(lax.broadcasted_iota(jnp.int32, (2 * COLS, 2 * CZ), 1), CX - 1)

    @pl.loop(k * (chunk // GX), (k + 1) * (chunk // GX))
    def _(g):
        rows = []
        for i in range(GX):
            here = (lane2 == g * GX + i).astype(F32).astype(BF16)
            for y in range(0, CY, 2):
                rows.append(zc[pl.ds(COLS * y, 2 * COLS), :] * here)
        h = dot(jnp.concatenate(rows, axis=0), ez[...])
        for i in range(GX):
            x = g * GX + i
            for y in range(CY):
                q = (i * CY + y) * COLS
                s = jnp.broadcast_to(sbuf[x, pl.ds(y, 1), :], (COLS, CZ))
                obuf[x * CY + y] = obuf[x * CY + y] - s * h[q:q + COLS]


def trace_nodes(cells, vbuf, lane):
    def trace_one(k, acc):
        place = cells[0, k]
        row = vbuf[lax.shift_right_logical(place, 7)]
        turn = jnp.bitwise_and(k + CZ - jnp.bitwise_and(place, CZ - 1), CZ - 1)
        return jnp.where(lane == k, pltpu.roll(row, turn, 1), acc)

    return lax.fori_loop(0, BND, trace_one, jnp.zeros((COLS, CZ), F32), unroll=8)


def tile_products(xbuf, slots, rightb, leftb, nearb):
    pieces = []
    for j in range(TILES):
        xj = jnp.concatenate([xbuf[2 * j], xbuf[2 * j + 1]], axis=1)
        hi, lo = split(xj)
        pieces.append(jnp.concatenate([hi, lo], axis=0))
    xall = jnp.concatenate(pieces, axis=0).astype(BF16)
    lane2 = lax.broadcasted_iota(jnp.int32, (COLS, TB), 1)
    parts = []
    for i in range(ROWS):
        proj = dot_nt(xall, rightb[i])
        acc = jnp.zeros((COLS, TB), F32)
        chosen = jnp.zeros((2 * COLS, TB), F32)
        for j in range(TILES):
            far = jnp.where(slots[i, j] < 0, 1.0, 0.0).astype(F32)
            block = proj[16 * j:16 * j + 8] + proj[16 * j + 8:16 * j + 16]
            acc = jnp.where(lane2 // RANK == j, block * far, acc)
            chosen = chosen + pieces[j] * (1.0 - far)
        both = dot(stacked(acc), leftb[i]) + dot_nt(chosen.astype(BF16), nearb[i])
        parts.append(-(both[:COLS] + both[COLS:]))
    return jnp.concatenate(parts, axis=1)


def members(labels):
    which = lax.broadcasted_iota(jnp.int32, (CONDUCTORS, BND), 0)
    return (which == labels).astype(F32).astype(BF16)


def conductor_sums(values, onehots):
    both = dot_nt(stacked(values), onehots)
    return both[:COLS] + both[COLS:]


def conductor_weights(memb, slots, rightb, leftb, nearb, farl, nearl, wcon):
    lane = lax.broadcasted_iota(jnp.int32, (CONDUCTORS, TB), 1) // RANK
    side = CONDUCTORS * TILES
    for i in range(ROWS):
        cols = pl.ds(TB * i, TB)
        rows = memb[:, cols]
        pieces = [p.astype(BF16) for p in split(dot_nt(rows, leftb[i]))]
        for j in range(TILES):
            far = jnp.where(slots[i, j] < 0, 1.0, 0.0).astype(F32)
            mask = jnp.where(lane == j, far, 0.0).astype(BF16)
            for p in range(2):
                farl[pl.ds(side * p + CONDUCTORS * j, CONDUCTORS), cols] = pieces[p] * mask
            nearl[pl.ds(CONDUCTORS * j, CONDUCTORS), cols] = rows * jnp.full((CONDUCTORS, TB), 1.0 - far).astype(BF16)
    both = dot(farl[...], rightb[...].reshape(ROWS * TB, TB))
    total = both[:side] + both[side:] + dot(nearl[...], nearb[...].reshape(ROWS * TB, TB))
    for p, piece in enumerate(split(total)):
        wcon[pl.ds(side * p, side), :] = piece.astype(BF16)


def conductor_products(xbuf, wcon):
    total = jnp.zeros((2 * COLS, CONDUCTORS), F32)
    for j in range(TILES):
        xj = stacked(jnp.concatenate([xbuf[2 * j], xbuf[2 * j + 1]], axis=1))
        for p in range(2):
            total = total + dot_nt(xj, wcon[pl.ds(CONDUCTORS * (TILES * p + j), CONDUCTORS), :])
    return total[:COLS] + total[COLS:]


def kernel(
    vol, scal, diag, bnd, cell, lab, left, right, near, slot,
    obuf, bnd_out, charges,
    vbuf, wbuf, qbuf, lhs, sbuf, dbuf, bbuf, cellv, cells, labv, slots, leftb, rightb, nearb,
    xbuf, lbuf, memb, farl, nearl, wcon, ohz, wz, ez, zc, pbuf, rbuf, c1, c2, c3, c4, d1, zsend, zlo, zhi, trbuf,
    load_sem, vol_sem, xs_sem, xr_sem, ls_sem, lr_sem, hs_sem, hr_sem,
    ms_sem, mr_sem, zs_sem, zr_sem, cs_sem, cr_sem, ds_sem, dr_sem, hd_sem, hd_sem2,
):
    gx, gy, gz = lax.axis_index("gx"), lax.axis_index("gy"), lax.axis_index("gz")
    group = (gx * NY + gy) // 2
    pos = lax.rem(gy, 2) * NZ + gz
    own_group = group == gz
    lane = lax.broadcasted_iota(jnp.int32, (COLS, CZ), 1)

    def remote(src, dst, send_sem, recv_sem, device):
        return pltpu.make_async_remote_copy(src, dst, send_sem, recv_sem, device_id=device, device_id_type=MESH)

    def plane(a, b):
        return jnp.bitwise_xor(gx, a), lax.rem(gy + b, NY)

    def line(k):
        return gx, gy, jnp.bitwise_xor(gz, k)

    at_head = jnp.logical_and(gx == HEAD[0], jnp.logical_and(gy == HEAD[1], gz == HEAD[2]))
    away = jnp.logical_not(at_head)
    first = [(jnp.bitwise_xor(gx, a), gy, jnp.bitwise_xor(gz, b)) for a, b in FIRST]
    second = [(jnp.bitwise_xor(gx, 1), lax.rem(gy + b, NY), jnp.bitwise_xor(gz, 2 * c)) for b, c in SECOND]

    small = [(bnd, bbuf), (lab, labv), (cell, cells), (cell, cellv), (slot, slots),
             (scal, sbuf), (diag, dbuf), (right, rightb), (left, leftb), (near, nearb)]
    loads = [pltpu.make_async_copy(s, d, load_sem.at[i]) for i, (s, d) in enumerate(small)]
    (l_bnd, l_lab, l_cells, l_cellv, l_slot, l_scal, l_diag, l_right, l_left, l_near) = loads
    l_bnd.start()
    l_lab.start()

    for x in (0, CX + 1):
        wbuf[x] = jnp.zeros((CY + 2, COLS, CZ), F32)
    for y in (0, CY + 1):
        wbuf[:, y] = jnp.zeros((CX + 2, COLS, CZ), F32)
    zlo[...] = jnp.zeros_like(zlo)
    zhi[...] = jnp.zeros_like(zhi)

    barrier = pltpu.get_barrier_semaphore()

    def greet(device):
        pl.semaphore_signal(barrier, inc=1, device_id=device, device_id_type=MESH)

    for k in LINE + [0]:
        for p in range(2):
            source = (gz // 2, lax.rem(gz, 2) * 2 + p, jnp.bitwise_xor(gz, k))
            if k:
                greet(source)
            else:
                here = jnp.logical_and(own_group, lax.rem(gy, 2) == p)
                pl.when(jnp.logical_not(here))(functools.partial(greet, source))
    for device in second:
        greet(device)
    for k in LINE:
        greet(line(k))
    for device in first:
        greet(device)

    def within(a, b):
        return jnp.logical_and(jnp.logical_and(a >= 0, a < NX), jnp.logical_and(b >= 0, b < NY))

    halo = []
    count = GROUP - own_group.astype(jnp.int32) + len(SECOND) + len(LINE) + len(FIRST)
    for i, (dx, dy) in enumerate(NEIGHBOURS):
        (fx, tx), (fy, ty) = face(dx, CX), face(dy, CY)
        device = (lax.rem(gx + dx + NX, NX), lax.rem(gy + dy + NY, NY), gz)
        to, come = within(gx + dx, gy + dy), within(gx - dx, gy - dy)
        halo.append((remote(wbuf.at[fx, fy], wbuf.at[tx, ty], hs_sem.at[i], hr_sem.at[i], device), to, come))
        pl.when(to)(functools.partial(greet, device))
        count = count + come.astype(jnp.int32)

    @pl.when(at_head)
    def _():
        @pl.loop(0, NX * NY * NZ)
        def _(i):
            device = (i // (NY * NZ), lax.rem(i // NZ, NY), lax.rem(i, NZ))
            pl.when(i != (HEAD[0] * NY + HEAD[1]) * NZ + HEAD[2])(lambda: greet(device))

    count = count + away.astype(jnp.int32)

    l_scal.start()
    for c in range(COLS):
        pltpu.make_async_copy(vol.at[c], vbuf.at[:, c, :], vol_sem).start()
    for l in (l_cells, l_cellv, l_diag, l_slot, l_right, l_left, l_near):
        l.start()
    l_bnd.wait()
    l_lab.wait()
    pl.semaphore_wait(barrier, count)

    x_sends = [remote(bbuf, xbuf.at[pos], xs_sem.at[i], xr_sem, (*plane(a, b), group)) for i, (a, b) in enumerate(PLANE)]
    x_last = remote(bbuf, xbuf.at[pos], xs_sem.at[len(PLANE)], xr_sem, (gx, gy, group))
    x_self = pltpu.make_async_copy(bbuf, xbuf.at[pos], xr_sem)
    label_sends = [remote(labv, lbuf.at[gz], ls_sem, lr_sem, line(k)) for k in LINE]
    for s in x_sends[:2] + label_sends + x_sends[2:]:
        s.start()
    pl.when(jnp.logical_not(own_group))(x_last.start)
    pl.when(own_group)(x_self.start)
    lbuf[gz] = labv[...]

    l_scal.wait()
    pltpu.make_async_copy(vbuf, vbuf, vol_sem).wait()
    scale_pass(sbuf, vbuf, wbuf)
    for copy, to, come in halo:
        pl.when(to)(copy.start)

    l_cells.wait()
    l_cellv.wait()
    l_diag.wait()
    trbuf[...] = trace_nodes(cells, vbuf, lane)
    line_weights(wz, ez)
    node_columns(cellv, ohz)
    node_pass(bbuf, cellv, ohz, vbuf, dbuf, lhs, obuf)
    zsend[...] = jnp.zeros_like(zsend)
    c1[...] = jnp.zeros_like(c1)
    own_sums = conductor_sums(trbuf[...], members(labv[...]))

    pltpu.make_async_copy(lbuf.at[pl.ds(0, NZ - 1)], lbuf.at[pl.ds(0, NZ - 1)], lr_sem).wait()
    for b in range(NZ):
        memb[:, pl.ds(b * BND, BND)] = members(lbuf[b])

    l_slot.wait()
    l_right.wait()
    l_left.wait()
    l_near.wait()
    conductor_weights(memb, slots, rightb, leftb, nearb, farl, nearl, wcon)

    pltpu.make_async_copy(xbuf, xbuf, xr_sem).wait()
    c1[:, pl.ds(0, CONDUCTORS)] = own_sums - conductor_products(xbuf, wcon)
    place = gx * 2 + lax.rem(gz, 2)
    head_place = gy * 4 + gz // 2
    head_send = remote(c1, d1.at[head_place, place], hd_sem, hd_sem2, HEAD)
    pl.when(away)(head_send.start)
    first_sends = [remote(c1, c2.at[place], cs_sem, cr_sem, device) for device in first]
    for s in first_sends:
        s.start()
    c2[place] = c1[...]

    values = tile_products(xbuf, slots, rightb, leftb, nearb)
    for b in range(NZ):
        pbuf[b] = values[:, b * BND:(b + 1) * BND]
    row_sends = [remote(pbuf.at[jnp.bitwise_xor(gz, k)], rbuf.at[gz], ms_sem, mr_sem, line(k)) for k in LINE]
    for s in row_sends:
        s.start()
    rbuf[gz] = pbuf[gz]

    for copy, to, come in halo:
        pl.when(come)(copy.wait_recv)
    line_pass(wbuf, lhs, qbuf)
    sum_pass(lhs, wz, qbuf, sbuf, obuf, zsend, lane)
    up, down = gz + 1 < NZ, gz > 0
    z_up = remote(zsend, zlo, zs_sem.at[0], zr_sem.at[0], (gx, gy, lax.rem(gz + 1, NZ)))
    z_down = remote(zsend, zhi, zs_sem.at[1], zr_sem.at[1], (gx, gy, lax.rem(gz + NZ - 1, NZ)))
    pl.when(up)(z_up.start)
    pl.when(down)(z_down.start)

    pltpu.make_async_copy(c2.at[pl.ds(0, len(FIRST))], c2.at[pl.ds(0, len(FIRST))], cr_sem).wait()
    c3[...] = total_of(c2)
    place = gy * 4 + gz // 2
    second_sends = []
    for i, (device, (b, c)) in enumerate(zip(second, SECOND)):
        to_head = jnp.logical_and(
            jnp.logical_and(gx == HEAD[0] ^ 1, gy == (HEAD[1] - b) % NY), gz == HEAD[2] ^ (2 * c))
        second_sends.append((remote(c3, c4.at[place], ds_sem.at[i], dr_sem, device), jnp.logical_not(to_head)))
    for s, to in second_sends:
        pl.when(to)(s.start)
    c4[place] = c3[...]

    pltpu.make_async_copy(rbuf.at[pl.ds(0, NZ - 1)], rbuf.at[pl.ds(0, NZ - 1)], mr_sem).wait()
    bnd_out[...] = trbuf[...] + total_of(rbuf)
    pl.when(down)(z_up.wait_recv)
    pl.when(up)(z_down.wait_recv)
    end_rows(zlo, zhi, zc, lane)
    end_pass(0, CX, zc, ez, sbuf, obuf)

    for s in x_sends + label_sends + first_sends + row_sends:
        s.wait_send()
    for s, to in second_sends:
        pl.when(to)(s.wait_send)
    pl.when(away)(head_send.wait_send)
    pl.when(jnp.logical_not(own_group))(x_last.wait_send)
    for copy, to, come in halo:
        pl.when(to)(copy.wait_send)
    pl.when(up)(z_up.wait_send)
    pl.when(down)(z_down.wait_send)

    scale = (CONDUCTORS / (BND * NX * NY * NZ)) ** 0.5

    @pl.when(away)
    def _():
        pltpu.make_async_copy(c4.at[pl.ds(0, len(SECOND))], c4.at[pl.ds(0, len(SECOND))], dr_sem).wait()
        charges[...] = total_of(c4)[:, :CONDUCTORS] * scale

    @pl.when(at_head)
    def _():
        d1[HEAD[1] * 4 + HEAD[2] // 2, HEAD[0] * 2 + HEAD[2] % 2] = c1[...]
        rest = d1.reshape(NX * NY * NZ, COLS, BND).at[pl.ds(0, NX * NY * NZ - 1)]
        pltpu.make_async_copy(rest, rest, hd_sem2).wait()
        for k in range(len(SECOND) + 1):
            c4[k] = total_of(d1.at[k])
        charges[...] = total_of(c4)[:, :CONDUCTORS] * scale


def deliver(field, rows, sums, out, bnd_out, charges, sem, small_sem):
    copies = [pltpu.make_async_copy(field.at[:, c, :], out.at[c], sem) for c in range(COLS)]
    copies.append(pltpu.make_async_copy(rows, bnd_out, small_sem.at[0]))
    copies.append(pltpu.make_async_copy(sums, charges, small_sem.at[1]))
    for c in copies:
        c.start()
    pltpu.make_async_copy(field, field, sem).wait()
    copies[-2].wait()
    copies[-1].wait()


def shards(vol, scal, diag, bnd, cell, lab, left, right, near, slot):
    nodes = CX * CY
    field = (nodes, COLS, CZ)
    dma = pltpu.SemaphoreType.DMA
    hbm_spec = pl.BlockSpec(memory_space=pltpu.HBM)
    vmem_spec = pl.BlockSpec(memory_space=pltpu.VMEM)
    operands = (
        vol.reshape(COLS, nodes, CZ), scal, diag, bnd, cell.reshape(1, BND), lab.reshape(1, BND),
        left.reshape(ROWS, TB, TB), right.reshape(ROWS, TB, TB), near.reshape(ROWS, TB, TB), slot,
    )
    operands = [pltpu.with_memory_space_constraint(o, pltpu.HBM) for o in operands]
    results = pl.pallas_call(
        kernel,
        out_shape=(
            pltpu.VMEM(field, F32),
            pltpu.VMEM((COLS, BND), F32),
            pltpu.VMEM((COLS, CONDUCTORS), F32),
        ),
        in_specs=[hbm_spec] * len(operands),
        out_specs=(vmem_spec,) * 3,
        scratch_shapes=[
            pltpu.VMEM(field, F32),
            pltpu.VMEM((CX + 2, CY + 2, COLS, CZ), F32),
            pltpu.VMEM(field, F32),
            pltpu.VMEM((CX, CY * COLS, 2 * CZ), BF16),
            pltpu.VMEM((CX, CY, CZ), F32),
            pltpu.VMEM((CX, CY, CZ), F32),
            pltpu.VMEM((COLS, BND), F32),
            pltpu.VMEM((1, BND), jnp.int32),
            pltpu.SMEM((1, BND), jnp.int32),
            pltpu.VMEM((1, BND), jnp.int32),
            pltpu.SMEM((ROWS, TILES), jnp.int32),
            pltpu.VMEM((ROWS, TB, TB), BF16),
            pltpu.VMEM((ROWS, TB, TB), BF16),
            pltpu.VMEM((ROWS, TB, TB), BF16),
            pltpu.VMEM((GROUP, COLS, BND), F32),
            pltpu.VMEM((NZ, 1, BND), jnp.int32),
            pltpu.VMEM((CONDUCTORS, NZ * BND), BF16),
            pltpu.VMEM((2 * CONDUCTORS * TILES, ROWS * TB), BF16),
            pltpu.VMEM((CONDUCTORS * TILES, ROWS * TB), BF16),
            pltpu.VMEM((2 * CONDUCTORS * TILES, TB), BF16),
            pltpu.VMEM((CZ, 2 * BND), BF16),
            pltpu.VMEM((2 * CZ, 2 * CZ), BF16),
            pltpu.VMEM((2 * CZ, CZ), BF16),
            pltpu.VMEM((CY * COLS, 2 * CZ), BF16),
            pltpu.VMEM((NZ, COLS, BND), F32),
            pltpu.VMEM((NZ, COLS, BND), F32),
            pltpu.VMEM((COLS, BND), F32),
            pltpu.VMEM((len(FIRST) + 1, COLS, BND), F32),
            pltpu.VMEM((COLS, BND), F32),
            pltpu.VMEM((len(SECOND) + 1, COLS, BND), F32),
            pltpu.VMEM((len(SECOND) + 1, len(FIRST) + 1, COLS, BND), F32),
            pltpu.VMEM((CY // 2, COLS, CZ), F32),
            pltpu.VMEM((CY // 2, COLS, CZ), F32),
            pltpu.VMEM((CY // 2, COLS, CZ), F32),
            pltpu.VMEM((COLS, BND), F32),
            dma((10,)), dma, dma((GROUP,)), dma, dma, dma, dma((8,)), dma((8,)),
            dma, dma, dma((2,)), dma((2,)), dma, dma, dma((len(SECOND),)), dma, dma, dma,
        ],
        compiler_params=pltpu.CompilerParams(
            collective_id=0, has_side_effects=True, vmem_limit_bytes=40 * 1024 * 1024),
    )(*operands)
    out, bnd_out, charges = pl.pallas_call(
        deliver,
        out_shape=(
            pltpu.HBM((COLS, nodes, CZ), F32),
            pltpu.HBM((COLS, BND), F32),
            pltpu.HBM((COLS, CONDUCTORS), F32),
        ),
        in_specs=[vmem_spec] * 3,
        out_specs=(hbm_spec,) * 3,
        scratch_shapes=[dma, dma((2,))],
    )(*[pltpu.with_memory_space_constraint(r, pltpu.VMEM) for r in results])
    return out.reshape(vol.shape), bnd_out, charges.T


def solution(mesh):
    in_specs = (
        P(None, "gx", "gy", "gz"),
        P("gx", "gy", "gz"),
        P("gx", "gy", "gz"),
        P(None, ("gx", "gy", "gz")),
        P(("gx", "gy", "gz")),
        P(("gx", "gy", "gz")),
        P(("gx", "gy"), "gz", None, None),
        P(("gx", "gy"), "gz", None, None),
        P(("gx", "gy"), "gz", None, None),
        P(("gx", "gy"), "gz"),
    )
    out_specs = (P(None, "gx", "gy", "gz"), P(None, ("gx", "gy", "gz")), P())
    return jax.shard_map(shards, mesh=mesh, in_specs=in_specs, out_specs=out_specs, check_vma=False)
```

```python
import functools

import jax
import jax.numpy as jnp
from jax import lax
from jax.experimental import pallas as pl
from jax.experimental.pallas import tpu as pltpu
from jax.sharding import PartitionSpec as P

MESH = pl.DeviceIdType.MESH
F32 = jnp.float32
BF16 = jnp.bfloat16

NX, NY, NZ = 4, 4, 8
PEERS = NX * NY
COLS, CX, CY, CZ = 8, 32, 16, 128
ROWS, TILES, RANK, TB = 4, 8, 32, 256
CONDUCTORS = 32
BND = 128
GROUP = PEERS
PLANE = [(3, 2), (2, 2), (3, 1), (3, 3), (2, 1), (2, 3), (1, 2), (0, 2), (3, 0), (2, 0), (1, 1), (1, 3), (0, 1), (0, 3), (1, 0)]
LINE = [5, 4, 7, 3, 6, 2, 1]
FIRST = [(3, 0), (2, 0), (3, 1), (2, 1), (1, 1), (0, 1), (1, 0)]
SECOND = [(2, 2), (2, 1), (2, 3), (1, 2), (3, 2), (2, 0), (0, 2), (1, 1), (1, 3), (3, 1), (3, 3), (1, 0), (3, 0), (0, 1), (0, 3)]
HEAD = (1, 0, 0)
NEIGHBOURS = [(dx, dy) for dx in (-1, 0, 1) for dy in (-1, 0, 1) if (dx, dy) != (0, 0)]


def split(x):
    hi = x.astype(BF16).astype(F32)
    return hi, x - hi


def stacked(x):
    hi, lo = split(x)
    return jnp.concatenate([hi, lo], axis=0).astype(BF16)


def dot(a, b):
    return lax.dot_general(a, b, (((1,), (0,)), ((), ())), preferred_element_type=F32)


def dot_nt(a, b):
    return lax.dot_general(a, b, (((1,), (1,)), ((), ())), preferred_element_type=F32)


def total_of(buf):
    parts = [buf[i] for i in range(buf.shape[0])]
    while len(parts) > 1:
        parts = [a + b for a, b in zip(parts[::2], parts[1::2])]
    return parts[0]


def face(step, size):
    if step == 0:
        return pl.ds(1, size), pl.ds(1, size)
    return (pl.ds(size, 1), pl.ds(0, 1)) if step > 0 else (pl.ds(1, 1), pl.ds(size + 1, 1))


GX = 8


def scale_pass(sbuf, vbuf, wbuf):
    @pl.loop(0, CX)
    def _(x):
        for y in range(CY):
            s = sbuf[x, pl.ds(y, 1), :] * (1.0 / 6.0)
            wbuf[x + 1, y + 1] = jnp.broadcast_to(s, (COLS, CZ)) * vbuf[x * CY + y]


def line_weights(wz, ez):
    z = lax.broadcasted_iota(jnp.int32, (CZ, CZ), 0)
    n = lax.broadcasted_iota(jnp.int32, (CZ, CZ), 1)
    near = jnp.logical_or(z == n + 1, z == n - 1)
    first = jnp.bitwise_and(n, CX) == 0
    ends = jnp.logical_or(jnp.logical_and(z == 0, first), jnp.logical_and(z == CZ - 1, jnp.logical_not(first)))
    from_above = jnp.bitwise_and(z, CX) == 0
    land = jnp.logical_or(jnp.logical_and(n == CZ - 1, from_above), jnp.logical_and(n == 0, jnp.logical_not(from_above)))

    def ones(mask):
        return mask.astype(F32).astype(BF16)

    for piece in range(2):
        rows = pl.ds(piece * CZ, CZ)
        wz[rows, pl.ds(0, CZ)] = ones(near)
        wz[rows, pl.ds(CZ, CZ)] = ones(ends)
        ez[rows, :] = ones(land)


def node_columns(cellv, ohz):
    zk = jnp.bitwise_and(cellv[...], CZ - 1)
    onehot = (lax.broadcasted_iota(jnp.int32, (CZ, BND), 0) == zk).astype(F32).astype(BF16)
    ohz[:, pl.ds(0, BND)] = onehot
    ohz[:, pl.ds(BND, BND)] = onehot


def node_pass(bbuf, cellv, ohz, vbuf, dbuf, lhs, obuf):
    spots = jnp.broadcast_to(lax.shift_right_logical(cellv[...], 7), (COLS, BND))
    pieces = split(bbuf[...])

    @pl.loop(0, CX)
    def _(x):
        for y in range(0, CY, 2):
            here = [spots == x * CY + y, spots == x * CY + y + 1]
            for p in range(2):
                both = jnp.concatenate([jnp.where(h, pieces[p], 0.0) for h in here], axis=0)
                lhs[x, pl.ds(COLS * y, 2 * COLS), pl.ds(p * BND, BND)] = both.astype(BF16)

    for g in range(CX // GX):
        extra = dot_nt(lhs[pl.ds(g * GX, GX)].reshape(GX * CY * COLS, 2 * BND), ohz[...])
        for i in range(GX):
            for y in range(CY):
                x = g * GX + i
                d = jnp.broadcast_to(dbuf[x, pl.ds(y, 1), :], (COLS, CZ))
                k = (i * CY + y) * COLS
                obuf[x * CY + y] = d * vbuf[x * CY + y] + extra[k:k + COLS]


def line_pass(wbuf, lhs, qbuf):
    @pl.loop(0, CX)
    def _(x):
        a = [wbuf[x, y] + wbuf[x + 2, y] for y in range(CY + 2)]
        w = [wbuf[x + 1, y] for y in range(CY + 2)]
        for y0 in range(0, CY, 2):
            ts = []
            for y in (y0, y0 + 1):
                p = a[y] + a[y + 2]
                ts.append((a[y + 1] + (w[y] + w[y + 2])) + 0.5 * p)
                qbuf[x * CY + y] = 16.0 * w[y + 1] - p
            t = jnp.concatenate(ts, axis=0)
            hi = t.astype(BF16)
            lhs[x, pl.ds(COLS * y0, 2 * COLS), pl.ds(0, CZ)] = hi
            lhs[x, pl.ds(COLS * y0, 2 * COLS), pl.ds(CZ, CZ)] = (t - hi.astype(F32)).astype(BF16)


def sum_pass(lhs, wz, qbuf, sbuf, obuf, zsend, lane):
    spot = jnp.bitwise_and(lane, CX - 1)
    half = lax.shift_right_logical(lane, 6)

    for g in range(CX // GX):
        r = dot(lhs[pl.ds(g * GX, GX)].reshape(GX * CY * COLS, 2 * CZ), wz[...])
        ends = [zsend[y] for y in range(CY // 2)]
        for i in range(GX):
            x = g * GX + i
            mine = [jnp.logical_and(half == h, spot == x) for h in range(2)]
            for y in range(CY):
                k = (i * CY + y) * COLS
                s = jnp.broadcast_to(sbuf[x, pl.ds(y, 1), :], (COLS, CZ))
                obuf[x * CY + y] = obuf[x * CY + y] + s * (qbuf[x * CY + y] - r[k:k + COLS, :CZ])
                e = y % (CY // 2)
                ends[e] = jnp.where(mine[y // (CY // 2)], r[k:k + COLS, CZ:], ends[e])
        for y in range(CY // 2):
            zsend[y] = ends[y]


def end_rows(zlo, zhi, zc, lane):
    above = jnp.bitwise_and(lane, CX) == 0
    for y in range(0, CY, 2):
        e = y % (CY // 2)
        both = []
        for k in (e, e + 1):
            row = jnp.where(above, zhi[k], zlo[k])
            both.append(jnp.where(lax.shift_right_logical(lane, 6) == y // (CY // 2), row, 0.0))
        z = jnp.concatenate(both, axis=0)
        hi = z.astype(BF16)
        zc[pl.ds(COLS * y, 2 * COLS), pl.ds(0, CZ)] = hi
        zc[pl.ds(COLS * y, 2 * COLS), pl.ds(CZ, CZ)] = (z - hi.astype(F32)).astype(BF16)


def end_pass(zc, ez, sbuf, obuf):
    lane2 = jnp.bitwise_and(lax.broadcasted_iota(jnp.int32, (2 * COLS, 2 * CZ), 1), CX - 1)

    for g in range(CX // GX):
        rows = []
        for i in range(GX):
            here = (lane2 == g * GX + i).astype(F32).astype(BF16)
            for y in range(0, CY, 2):
                rows.append(zc[pl.ds(COLS * y, 2 * COLS), :] * here)
        h = dot(jnp.concatenate(rows, axis=0), ez[...])
        for i in range(GX):
            x = g * GX + i
            for y in range(CY):
                q = (i * CY + y) * COLS
                s = jnp.broadcast_to(sbuf[x, pl.ds(y, 1), :], (COLS, CZ))
                obuf[x * CY + y] = obuf[x * CY + y] - s * h[q:q + COLS]


def trace_nodes(cells, vbuf, lane):
    def trace_one(k, acc):
        place = cells[0, k]
        row = vbuf[lax.shift_right_logical(place, 7)]
        turn = jnp.bitwise_and(k + CZ - jnp.bitwise_and(place, CZ - 1), CZ - 1)
        return jnp.where(lane == k, pltpu.roll(row, turn, 1), acc)

    return lax.fori_loop(0, BND, trace_one, jnp.zeros((COLS, CZ), F32), unroll=8)


def tile_products(xbuf, slots, rightb, leftb, nearb):
    pieces = []
    for j in range(TILES):
        xj = jnp.concatenate([xbuf[2 * j], xbuf[2 * j + 1]], axis=1)
        hi, lo = split(xj)
        pieces.append(jnp.concatenate([hi, lo], axis=0))
    xall = jnp.concatenate(pieces, axis=0).astype(BF16)
    lane2 = lax.broadcasted_iota(jnp.int32, (COLS, TB), 1)
    parts = []
    for i in range(ROWS):
        proj = dot_nt(xall, rightb[i])
        acc = jnp.zeros((COLS, TB), F32)
        chosen = jnp.zeros((2 * COLS, TB), F32)
        for j in range(TILES):
            far = jnp.where(slots[i, j] < 0, 1.0, 0.0).astype(F32)
            block = proj[16 * j:16 * j + 8] + proj[16 * j + 8:16 * j + 16]
            acc = jnp.where(lane2 // RANK == j, block * far, acc)
            chosen = chosen + pieces[j] * (1.0 - far)
        both = dot(stacked(acc), leftb[i]) + dot_nt(chosen.astype(BF16), nearb[i])
        parts.append(-(both[:COLS] + both[COLS:]))
    return jnp.concatenate(parts, axis=1)


def members(labels):
    which = lax.broadcasted_iota(jnp.int32, (CONDUCTORS, BND), 0)
    return (which == labels).astype(F32).astype(BF16)


def conductor_sums(values, onehots):
    both = dot_nt(stacked(values), onehots)
    return both[:COLS] + both[COLS:]


def conductor_weights(memb, slots, rightb, leftb, nearb, farl, nearl, wcon):
    lane = lax.broadcasted_iota(jnp.int32, (CONDUCTORS, TB), 1) // RANK
    side = CONDUCTORS * TILES
    for i in range(ROWS):
        cols = pl.ds(TB * i, TB)
        rows = memb[:, cols]
        pieces = [p.astype(BF16) for p in split(dot_nt(rows, leftb[i]))]
        for j in range(TILES):
            far = jnp.where(slots[i, j] < 0, 1.0, 0.0).astype(F32)
            mask = jnp.where(lane == j, far, 0.0).astype(BF16)
            for p in range(2):
                farl[pl.ds(side * p + CONDUCTORS * j, CONDUCTORS), cols] = pieces[p] * mask
            nearl[pl.ds(CONDUCTORS * j, CONDUCTORS), cols] = rows * jnp.full((CONDUCTORS, TB), 1.0 - far).astype(BF16)
    both = dot(farl[...], rightb[...].reshape(ROWS * TB, TB))
    total = both[:side] + both[side:] + dot(nearl[...], nearb[...].reshape(ROWS * TB, TB))
    for p, piece in enumerate(split(total)):
        wcon[pl.ds(side * p, side), :] = piece.astype(BF16)


def conductor_products(xbuf, wcon):
    total = jnp.zeros((2 * COLS, CONDUCTORS), F32)
    for j in range(TILES):
        xj = stacked(jnp.concatenate([xbuf[2 * j], xbuf[2 * j + 1]], axis=1))
        for p in range(2):
            total = total + dot_nt(xj, wcon[pl.ds(CONDUCTORS * (TILES * p + j), CONDUCTORS), :])
    return total[:COLS] + total[COLS:]


def kernel(
    vol, scal, diag, bnd, cell, lab, left, right, near, slot,
    obuf, bnd_out, charges,
    vbuf, wbuf, qbuf, lhs, sbuf, dbuf, bbuf, cellv, cells, labv, slots, leftb, rightb, nearb,
    xbuf, lbuf, memb, farl, nearl, wcon, ohz, wz, ez, zc, pbuf, rbuf, c1, c2, c3, c4, d1, zsend, zlo, zhi, trbuf,
    load_sem, vol_sem, xs_sem, xr_sem, ls_sem, lr_sem, hs_sem, hr_sem,
    ms_sem, mr_sem, zs_sem, zr_sem, cs_sem, cr_sem, ds_sem, dr_sem, hd_sem, hd_sem2,
):
    gx, gy, gz = lax.axis_index("gx"), lax.axis_index("gy"), lax.axis_index("gz")
    group = (gx * NY + gy) // 2
    pos = lax.rem(gy, 2) * NZ + gz
    own_group = group == gz
    lane = lax.broadcasted_iota(jnp.int32, (COLS, CZ), 1)

    def remote(src, dst, send_sem, recv_sem, device):
        return pltpu.make_async_remote_copy(src, dst, send_sem, recv_sem, device_id=device, device_id_type=MESH)

    def plane(a, b):
        return jnp.bitwise_xor(gx, a), lax.rem(gy + b, NY)

    def line(k):
        return gx, gy, jnp.bitwise_xor(gz, k)

    at_head = jnp.logical_and(gx == HEAD[0], jnp.logical_and(gy == HEAD[1], gz == HEAD[2]))
    away = jnp.logical_not(at_head)
    first = [(jnp.bitwise_xor(gx, a), gy, jnp.bitwise_xor(gz, b)) for a, b in FIRST]
    second = [(jnp.bitwise_xor(gx, 1), lax.rem(gy + b, NY), jnp.bitwise_xor(gz, 2 * c)) for b, c in SECOND]

    small = [(bnd, bbuf), (lab, labv), (cell, cells), (cell, cellv), (slot, slots),
             (scal, sbuf), (diag, dbuf), (right, rightb), (left, leftb), (near, nearb)]
    loads = [pltpu.make_async_copy(s, d, load_sem.at[i]) for i, (s, d) in enumerate(small)]
    (l_bnd, l_lab, l_cells, l_cellv, l_slot, l_scal, l_diag, l_right, l_left, l_near) = loads
    l_bnd.start()
    l_lab.start()

    for x in (0, CX + 1):
        wbuf[x] = jnp.zeros((CY + 2, COLS, CZ), F32)
    for y in (0, CY + 1):
        wbuf[:, y] = jnp.zeros((CX + 2, COLS, CZ), F32)
    zlo[...] = jnp.zeros_like(zlo)
    zhi[...] = jnp.zeros_like(zhi)

    barrier = pltpu.get_barrier_semaphore()

    def greet(device):
        pl.semaphore_signal(barrier, inc=1, device_id=device, device_id_type=MESH)

    for k in LINE + [0]:
        for p in range(2):
            source = (gz // 2, lax.rem(gz, 2) * 2 + p, jnp.bitwise_xor(gz, k))
            if k:
                greet(source)
            else:
                here = jnp.logical_and(own_group, lax.rem(gy, 2) == p)
                pl.when(jnp.logical_not(here))(functools.partial(greet, source))
    for device in second:
        greet(device)
    for k in LINE:
        greet(line(k))
    for device in first:
        greet(device)

    def within(a, b):
        return jnp.logical_and(jnp.logical_and(a >= 0, a < NX), jnp.logical_and(b >= 0, b < NY))

    halo = []
    count = GROUP - own_group.astype(jnp.int32) + len(SECOND) + len(LINE) + len(FIRST)
    for i, (dx, dy) in enumerate(NEIGHBOURS):
        (fx, tx), (fy, ty) = face(dx, CX), face(dy, CY)
        device = (lax.rem(gx + dx + NX, NX), lax.rem(gy + dy + NY, NY), gz)
        to, come = within(gx + dx, gy + dy), within(gx - dx, gy - dy)
        halo.append((remote(wbuf.at[fx, fy], wbuf.at[tx, ty], hs_sem.at[i], hr_sem.at[i], device), to, come))
        pl.when(to)(functools.partial(greet, device))
        count = count + come.astype(jnp.int32)

    @pl.when(at_head)
    def _():
        @pl.loop(0, NX * NY * NZ)
        def _(i):
            device = (i // (NY * NZ), lax.rem(i // NZ, NY), lax.rem(i, NZ))
            pl.when(i != (HEAD[0] * NY + HEAD[1]) * NZ + HEAD[2])(lambda: greet(device))

    count = count + away.astype(jnp.int32)

    l_scal.start()
    for c in range(COLS):
        pltpu.make_async_copy(vol.at[c], vbuf.at[:, c, :], vol_sem).start()
    for l in (l_cells, l_cellv, l_diag, l_slot, l_right, l_left, l_near):
        l.start()
    l_bnd.wait()
    l_lab.wait()
    pl.semaphore_wait(barrier, count)

    x_sends = [remote(bbuf, xbuf.at[pos], xs_sem.at[i], xr_sem, (*plane(a, b), group)) for i, (a, b) in enumerate(PLANE)]
    x_last = remote(bbuf, xbuf.at[pos], xs_sem.at[len(PLANE)], xr_sem, (gx, gy, group))
    x_self = pltpu.make_async_copy(bbuf, xbuf.at[pos], xr_sem)
    label_sends = [remote(labv, lbuf.at[gz], ls_sem, lr_sem, line(k)) for k in LINE]
    for s in x_sends[:2] + label_sends + x_sends[2:]:
        s.start()
    pl.when(jnp.logical_not(own_group))(x_last.start)
    pl.when(own_group)(x_self.start)
    lbuf[gz] = labv[...]

    l_scal.wait()
    pltpu.make_async_copy(vbuf, vbuf, vol_sem).wait()
    scale_pass(sbuf, vbuf, wbuf)
    for copy, to, come in halo:
        pl.when(to)(copy.start)

    l_cells.wait()
    l_cellv.wait()
    l_diag.wait()
    trbuf[...] = trace_nodes(cells, vbuf, lane)
    line_weights(wz, ez)
    node_columns(cellv, ohz)
    node_pass(bbuf, cellv, ohz, vbuf, dbuf, lhs, obuf)
    zsend[...] = jnp.zeros_like(zsend)
    c1[...] = jnp.zeros_like(c1)
    own_sums = conductor_sums(trbuf[...], members(labv[...]))

    pltpu.make_async_copy(lbuf.at[pl.ds(0, NZ - 1)], lbuf.at[pl.ds(0, NZ - 1)], lr_sem).wait()
    for b in range(NZ):
        memb[:, pl.ds(b * BND, BND)] = members(lbuf[b])

    l_slot.wait()
    l_right.wait()
    l_left.wait()
    l_near.wait()
    conductor_weights(memb, slots, rightb, leftb, nearb, farl, nearl, wcon)

    pltpu.make_async_copy(xbuf, xbuf, xr_sem).wait()
    c1[:, pl.ds(0, CONDUCTORS)] = own_sums - conductor_products(xbuf, wcon)
    place = gx * 2 + lax.rem(gz, 2)
    head_place = gy * 4 + gz // 2
    head_send = remote(c1, d1.at[head_place, place], hd_sem, hd_sem2, HEAD)
    pl.when(away)(head_send.start)
    first_sends = [remote(c1, c2.at[place], cs_sem, cr_sem, device) for device in first]
    for s in first_sends:
        s.start()
    c2[place] = c1[...]

    values = tile_products(xbuf, slots, rightb, leftb, nearb)
    for b in range(NZ):
        pbuf[b] = values[:, b * BND:(b + 1) * BND]
    row_sends = [remote(pbuf.at[jnp.bitwise_xor(gz, k)], rbuf.at[gz], ms_sem, mr_sem, line(k)) for k in LINE]
    for s in row_sends:
        s.start()
    rbuf[gz] = pbuf[gz]

    for copy, to, come in halo:
        pl.when(come)(copy.wait_recv)
    line_pass(wbuf, lhs, qbuf)
    sum_pass(lhs, wz, qbuf, sbuf, obuf, zsend, lane)
    up, down = gz + 1 < NZ, gz > 0
    z_up = remote(zsend, zlo, zs_sem.at[0], zr_sem.at[0], (gx, gy, lax.rem(gz + 1, NZ)))
    z_down = remote(zsend, zhi, zs_sem.at[1], zr_sem.at[1], (gx, gy, lax.rem(gz + NZ - 1, NZ)))
    pl.when(up)(z_up.start)
    pl.when(down)(z_down.start)

    pltpu.make_async_copy(c2.at[pl.ds(0, len(FIRST))], c2.at[pl.ds(0, len(FIRST))], cr_sem).wait()
    c3[...] = total_of(c2)
    place = gy * 4 + gz // 2
    second_sends = []
    for i, (device, (b, c)) in enumerate(zip(second, SECOND)):
        to_head = jnp.logical_and(
            jnp.logical_and(gx == HEAD[0] ^ 1, gy == (HEAD[1] - b) % NY), gz == HEAD[2] ^ (2 * c))
        second_sends.append((remote(c3, c4.at[place], ds_sem.at[i], dr_sem, device), jnp.logical_not(to_head)))
    for s, to in second_sends:
        pl.when(to)(s.start)
    c4[place] = c3[...]

    pltpu.make_async_copy(rbuf.at[pl.ds(0, NZ - 1)], rbuf.at[pl.ds(0, NZ - 1)], mr_sem).wait()
    bnd_out[...] = trbuf[...] + total_of(rbuf)
    pl.when(down)(z_up.wait_recv)
    pl.when(up)(z_down.wait_recv)
    end_rows(zlo, zhi, zc, lane)
    end_pass(zc, ez, sbuf, obuf)

    for s in x_sends + label_sends + first_sends + row_sends:
        s.wait_send()
    for s, to in second_sends:
        pl.when(to)(s.wait_send)
    pl.when(away)(head_send.wait_send)
    pl.when(jnp.logical_not(own_group))(x_last.wait_send)
    for copy, to, come in halo:
        pl.when(to)(copy.wait_send)
    pl.when(up)(z_up.wait_send)
    pl.when(down)(z_down.wait_send)

    scale = (CONDUCTORS / (BND * NX * NY * NZ)) ** 0.5

    @pl.when(away)
    def _():
        pltpu.make_async_copy(c4.at[pl.ds(0, len(SECOND))], c4.at[pl.ds(0, len(SECOND))], dr_sem).wait()
        charges[...] = total_of(c4)[:, :CONDUCTORS] * scale

    @pl.when(at_head)
    def _():
        d1[HEAD[1] * 4 + HEAD[2] // 2, HEAD[0] * 2 + HEAD[2] % 2] = c1[...]
        rest = d1.reshape(NX * NY * NZ, COLS, BND).at[pl.ds(0, NX * NY * NZ - 1)]
        pltpu.make_async_copy(rest, rest, hd_sem2).wait()
        for k in range(len(SECOND) + 1):
            c4[k] = total_of(d1.at[k])
        charges[...] = total_of(c4)[:, :CONDUCTORS] * scale


def deliver(field, rows, sums, out, bnd_out, charges, sem, small_sem):
    copies = [pltpu.make_async_copy(field.at[:, c, :], out.at[c], sem) for c in range(COLS)]
    copies.append(pltpu.make_async_copy(rows, bnd_out, small_sem.at[0]))
    copies.append(pltpu.make_async_copy(sums, charges, small_sem.at[1]))
    for c in copies:
        c.start()
    pltpu.make_async_copy(field, field, sem).wait()
    copies[-2].wait()
    copies[-1].wait()


def shards(vol, scal, diag, bnd, cell, lab, left, right, near, slot):
    nodes = CX * CY
    field = (nodes, COLS, CZ)
    dma = pltpu.SemaphoreType.DMA
    hbm_spec = pl.BlockSpec(memory_space=pltpu.HBM)
    vmem_spec = pl.BlockSpec(memory_space=pltpu.VMEM)
    operands = (
        vol.reshape(COLS, nodes, CZ), scal, diag, bnd, cell.reshape(1, BND), lab.reshape(1, BND),
        left.reshape(ROWS, TB, TB), right.reshape(ROWS, TB, TB), near.reshape(ROWS, TB, TB), slot,
    )
    operands = [pltpu.with_memory_space_constraint(o, pltpu.HBM) for o in operands]
    results = pl.pallas_call(
        kernel,
        out_shape=(
            pltpu.VMEM(field, F32),
            pltpu.VMEM((COLS, BND), F32),
            pltpu.VMEM((COLS, CONDUCTORS), F32),
        ),
        in_specs=[hbm_spec] * len(operands),
        out_specs=(vmem_spec,) * 3,
        scratch_shapes=[
            pltpu.VMEM(field, F32),
            pltpu.VMEM((CX + 2, CY + 2, COLS, CZ), F32),
            pltpu.VMEM(field, F32),
            pltpu.VMEM((CX, CY * COLS, 2 * CZ), BF16),
            pltpu.VMEM((CX, CY, CZ), F32),
            pltpu.VMEM((CX, CY, CZ), F32),
            pltpu.VMEM((COLS, BND), F32),
            pltpu.VMEM((1, BND), jnp.int32),
            pltpu.SMEM((1, BND), jnp.int32),
            pltpu.VMEM((1, BND), jnp.int32),
            pltpu.SMEM((ROWS, TILES), jnp.int32),
            pltpu.VMEM((ROWS, TB, TB), BF16),
            pltpu.VMEM((ROWS, TB, TB), BF16),
            pltpu.VMEM((ROWS, TB, TB), BF16),
            pltpu.VMEM((GROUP, COLS, BND), F32),
            pltpu.VMEM((NZ, 1, BND), jnp.int32),
            pltpu.VMEM((CONDUCTORS, NZ * BND), BF16),
            pltpu.VMEM((2 * CONDUCTORS * TILES, ROWS * TB), BF16),
            pltpu.VMEM((CONDUCTORS * TILES, ROWS * TB), BF16),
            pltpu.VMEM((2 * CONDUCTORS * TILES, TB), BF16),
            pltpu.VMEM((CZ, 2 * BND), BF16),
            pltpu.VMEM((2 * CZ, 2 * CZ), BF16),
            pltpu.VMEM((2 * CZ, CZ), BF16),
            pltpu.VMEM((CY * COLS, 2 * CZ), BF16),
            pltpu.VMEM((NZ, COLS, BND), F32),
            pltpu.VMEM((NZ, COLS, BND), F32),
            pltpu.VMEM((COLS, BND), F32),
            pltpu.VMEM((len(FIRST) + 1, COLS, BND), F32),
            pltpu.VMEM((COLS, BND), F32),
            pltpu.VMEM((len(SECOND) + 1, COLS, BND), F32),
            pltpu.VMEM((len(SECOND) + 1, len(FIRST) + 1, COLS, BND), F32),
            pltpu.VMEM((CY // 2, COLS, CZ), F32),
            pltpu.VMEM((CY // 2, COLS, CZ), F32),
            pltpu.VMEM((CY // 2, COLS, CZ), F32),
            pltpu.VMEM((COLS, BND), F32),
            dma((10,)), dma, dma((GROUP,)), dma, dma, dma, dma((8,)), dma((8,)),
            dma, dma, dma((2,)), dma((2,)), dma, dma, dma((len(SECOND),)), dma, dma, dma,
        ],
        compiler_params=pltpu.CompilerParams(
            collective_id=0, has_side_effects=True, vmem_limit_bytes=40 * 1024 * 1024),
    )(*operands)
    out, bnd_out, charges = pl.pallas_call(
        deliver,
        out_shape=(
            pltpu.HBM((COLS, nodes, CZ), F32),
            pltpu.HBM((COLS, BND), F32),
            pltpu.HBM((COLS, CONDUCTORS), F32),
        ),
        in_specs=[vmem_spec] * 3,
        out_specs=(hbm_spec,) * 3,
        scratch_shapes=[dma, dma((2,))],
    )(*[pltpu.with_memory_space_constraint(r, pltpu.VMEM) for r in results])
    return out.reshape(vol.shape), bnd_out, charges.T


def solution(mesh):
    in_specs = (
        P(None, "gx", "gy", "gz"),
        P("gx", "gy", "gz"),
        P("gx", "gy", "gz"),
        P(None, ("gx", "gy", "gz")),
        P(("gx", "gy", "gz")),
        P(("gx", "gy", "gz")),
        P(("gx", "gy"), "gz", None, None),
        P(("gx", "gy"), "gz", None, None),
        P(("gx", "gy"), "gz", None, None),
        P(("gx", "gy"), "gz"),
    )
    out_specs = (P(None, "gx", "gy", "gz"), P(None, ("gx", "gy", "gz")), P())
    return jax.shard_map(shards, mesh=mesh, in_specs=in_specs, out_specs=out_specs, check_vma=False)
```

```python
import functools

import jax
import jax.numpy as jnp
from jax import lax
from jax.experimental import pallas as pl
from jax.experimental.pallas import tpu as pltpu
from jax.sharding import PartitionSpec as P

MESH = pl.DeviceIdType.MESH
F32 = jnp.float32
BF16 = jnp.bfloat16

NX, NY, NZ = 4, 4, 8
PEERS = NX * NY
COLS, CX, CY, CZ = 8, 32, 16, 128
ROWS, TILES, RANK, TB = 4, 8, 32, 256
CONDUCTORS = 32
BND = 128
GROUP = PEERS
PLANE = [(3, 2), (2, 2), (3, 1), (3, 3), (2, 1), (2, 3), (1, 2), (0, 2), (3, 0), (2, 0), (1, 1), (1, 3), (0, 1), (0, 3), (1, 0)]
LINE = [5, 4, 7, 3, 6, 2, 1]
FIRST = [(3, 0), (2, 0), (3, 1), (2, 1), (1, 1), (0, 1), (1, 0)]
SECOND = [(2, 2), (2, 1), (2, 3), (1, 2), (3, 2), (2, 0), (0, 2), (1, 1), (1, 3), (3, 1), (3, 3), (1, 0), (3, 0), (0, 1), (0, 3)]
HEAD = (1, 0, 0)
NEIGHBOURS = [(dx, dy) for dx in (-1, 0, 1) for dy in (-1, 0, 1) if (dx, dy) != (0, 0)]


def split(x):
    hi = x.astype(BF16).astype(F32)
    return hi, x - hi


def stacked(x):
    hi, lo = split(x)
    return jnp.concatenate([hi, lo], axis=0).astype(BF16)


def dot(a, b):
    return lax.dot_general(a, b, (((1,), (0,)), ((), ())), preferred_element_type=F32)


def dot_nt(a, b):
    return lax.dot_general(a, b, (((1,), (1,)), ((), ())), preferred_element_type=F32)


def total_of(buf):
    parts = [buf[i] for i in range(buf.shape[0])]
    while len(parts) > 1:
        parts = [a + b for a, b in zip(parts[::2], parts[1::2])]
    return parts[0]


def face(step, size):
    if step == 0:
        return pl.ds(1, size), pl.ds(1, size)
    return (pl.ds(size, 1), pl.ds(0, 1)) if step > 0 else (pl.ds(1, 1), pl.ds(size + 1, 1))


GX = 8


def scale_pass(sbuf, vbuf, wbuf):
    @pl.loop(0, CX)
    def _(x):
        for y in range(CY):
            s = sbuf[x, pl.ds(y, 1), :] * (1.0 / 6.0)
            wbuf[x + 1, y + 1] = jnp.broadcast_to(s, (COLS, CZ)) * vbuf[x * CY + y]


def line_weights(wz, ez):
    z = lax.broadcasted_iota(jnp.int32, (CZ, CZ), 0)
    n = lax.broadcasted_iota(jnp.int32, (CZ, CZ), 1)
    near = jnp.logical_or(z == n + 1, z == n - 1)
    first = jnp.bitwise_and(n, CX) == 0
    ends = jnp.logical_or(jnp.logical_and(z == 0, first), jnp.logical_and(z == CZ - 1, jnp.logical_not(first)))
    from_above = jnp.bitwise_and(z, CX) == 0
    land = jnp.logical_or(jnp.logical_and(n == CZ - 1, from_above), jnp.logical_and(n == 0, jnp.logical_not(from_above)))

    def ones(mask):
        return mask.astype(F32).astype(BF16)

    for piece in range(2):
        rows = pl.ds(piece * CZ, CZ)
        wz[rows, pl.ds(0, CZ)] = ones(near)
        wz[rows, pl.ds(CZ, CZ)] = ones(ends)
        ez[rows, :] = ones(land)


def node_columns(cellv, ohz):
    zk = jnp.bitwise_and(cellv[...], CZ - 1)
    onehot = (lax.broadcasted_iota(jnp.int32, (CZ, BND), 0) == zk).astype(F32).astype(BF16)
    ohz[:, pl.ds(0, BND)] = onehot
    ohz[:, pl.ds(BND, BND)] = onehot


def node_pass(bbuf, cellv, ohz, vbuf, dbuf, lhs, obuf):
    spots = jnp.broadcast_to(lax.shift_right_logical(cellv[...], 7), (COLS, BND))
    pieces = split(bbuf[...])

    @pl.loop(0, CX)
    def _(x):
        for y in range(0, CY, 2):
            here = [spots == x * CY + y, spots == x * CY + y + 1]
            for p in range(2):
                both = jnp.concatenate([jnp.where(h, pieces[p], 0.0) for h in here], axis=0)
                lhs[x, pl.ds(COLS * y, 2 * COLS), pl.ds(p * BND, BND)] = both.astype(BF16)

    for g in range(CX // GX):
        extra = dot_nt(lhs[pl.ds(g * GX, GX)].reshape(GX * CY * COLS, 2 * BND), ohz[...])
        for i in range(GX):
            for y in range(CY):
                x = g * GX + i
                d = jnp.broadcast_to(dbuf[x, pl.ds(y, 1), :], (COLS, CZ))
                k = (i * CY + y) * COLS
                obuf[x * CY + y] = d * vbuf[x * CY + y] + extra[k:k + COLS]


def line_pass(wbuf, lhs, qbuf):
    @pl.loop(0, CX)
    def _(x):
        a = [wbuf[x, y] + wbuf[x + 2, y] for y in range(CY + 2)]
        w = [wbuf[x + 1, y] for y in range(CY + 2)]
        for y0 in range(0, CY, 2):
            ts = []
            for y in (y0, y0 + 1):
                p = a[y] + a[y + 2]
                ts.append((a[y + 1] + (w[y] + w[y + 2])) + 0.5 * p)
                qbuf[x * CY + y] = 16.0 * w[y + 1] - p
            t = jnp.concatenate(ts, axis=0)
            hi = t.astype(BF16)
            lhs[x, pl.ds(COLS * y0, 2 * COLS), pl.ds(0, CZ)] = hi
            lhs[x, pl.ds(COLS * y0, 2 * COLS), pl.ds(CZ, CZ)] = (t - hi.astype(F32)).astype(BF16)


def sum_pass(lhs, wz, qbuf, sbuf, obuf, zsend, lane):
    spot = jnp.bitwise_and(lane, CX - 1)
    half = lax.shift_right_logical(lane, 6)

    for g in range(CX // GX):
        r = dot(lhs[pl.ds(g * GX, GX)].reshape(GX * CY * COLS, 2 * CZ), wz[...])
        ends = [zsend[y] for y in range(CY // 2)]
        for i in range(GX):
            x = g * GX + i
            mine = [jnp.logical_and(half == h, spot == x) for h in range(2)]
            for y in range(CY):
                k = (i * CY + y) * COLS
                s = jnp.broadcast_to(sbuf[x, pl.ds(y, 1), :], (COLS, CZ))
                obuf[x * CY + y] = obuf[x * CY + y] + s * (qbuf[x * CY + y] - r[k:k + COLS, :CZ])
                e = y % (CY // 2)
                ends[e] = jnp.where(mine[y // (CY // 2)], r[k:k + COLS, CZ:], ends[e])
        for y in range(CY // 2):
            zsend[y] = ends[y]


def end_rows(zlo, zhi, zc, lane):
    above = jnp.bitwise_and(lane, CX) == 0
    for y in range(0, CY, 2):
        e = y % (CY // 2)
        both = []
        for k in (e, e + 1):
            row = jnp.where(above, zhi[k], zlo[k])
            both.append(jnp.where(lax.shift_right_logical(lane, 6) == y // (CY // 2), row, 0.0))
        z = jnp.concatenate(both, axis=0)
        hi = z.astype(BF16)
        zc[pl.ds(COLS * y, 2 * COLS), pl.ds(0, CZ)] = hi
        zc[pl.ds(COLS * y, 2 * COLS), pl.ds(CZ, CZ)] = (z - hi.astype(F32)).astype(BF16)


def end_pass(zc, ez, sbuf, obuf):
    lane2 = jnp.bitwise_and(lax.broadcasted_iota(jnp.int32, (2 * COLS, 2 * CZ), 1), CX - 1)

    for g in range(CX // GX):
        rows = []
        for i in range(GX):
            here = (lane2 == g * GX + i).astype(F32).astype(BF16)
            for y in range(0, CY, 2):
                rows.append(zc[pl.ds(COLS * y, 2 * COLS), :] * here)
        h = dot(jnp.concatenate(rows, axis=0), ez[...])
        for i in range(GX):
            x = g * GX + i
            for y in range(CY):
                q = (i * CY + y) * COLS
                s = jnp.broadcast_to(sbuf[x, pl.ds(y, 1), :], (COLS, CZ))
                obuf[x * CY + y] = obuf[x * CY + y] - s * h[q:q + COLS]


def trace_nodes(cells, vbuf, lane):
    def trace_one(k, acc):
        place = cells[0, k]
        row = vbuf[lax.shift_right_logical(place, 7)]
        turn = jnp.bitwise_and(k + CZ - jnp.bitwise_and(place, CZ - 1), CZ - 1)
        return jnp.where(lane == k, pltpu.roll(row, turn, 1), acc)

    return lax.fori_loop(0, BND, trace_one, jnp.zeros((COLS, CZ), F32), unroll=8)


def tile_products(xbuf, slots, rightb, leftb, nearb):
    pieces = []
    for j in range(TILES):
        xj = jnp.concatenate([xbuf[2 * j], xbuf[2 * j + 1]], axis=1)
        hi, lo = split(xj)
        pieces.append(jnp.concatenate([hi, lo], axis=0))
    xall = jnp.concatenate(pieces, axis=0).astype(BF16)
    lane2 = lax.broadcasted_iota(jnp.int32, (COLS, TB), 1)
    parts = []
    for i in range(ROWS):
        proj = dot_nt(xall, rightb[i])
        acc = jnp.zeros((COLS, TB), F32)
        chosen = jnp.zeros((2 * COLS, TB), F32)
        for j in range(TILES):
            far = jnp.where(slots[i, j] < 0, 1.0, 0.0).astype(F32)
            block = proj[16 * j:16 * j + 8] + proj[16 * j + 8:16 * j + 16]
            acc = jnp.where(lane2 // RANK == j, block * far, acc)
            chosen = chosen + pieces[j] * (1.0 - far)
        both = dot(stacked(acc), leftb[i]) + dot_nt(chosen.astype(BF16), nearb[i])
        parts.append(-(both[:COLS] + both[COLS:]))
    return jnp.concatenate(parts, axis=1)


def members(labels):
    which = lax.broadcasted_iota(jnp.int32, (CONDUCTORS, BND), 0)
    return (which == labels).astype(F32).astype(BF16)


def conductor_sums(values, onehots):
    both = dot_nt(stacked(values), onehots)
    return both[:COLS] + both[COLS:]


def conductor_weights(memb, slots, rightb, leftb, nearb, farl, nearl, wcon):
    lane = lax.broadcasted_iota(jnp.int32, (CONDUCTORS, TB), 1) // RANK
    side = CONDUCTORS * TILES
    for i in range(ROWS):
        cols = pl.ds(TB * i, TB)
        rows = memb[:, cols]
        pieces = [p.astype(BF16) for p in split(dot_nt(rows, leftb[i]))]
        for j in range(TILES):
            far = jnp.where(slots[i, j] < 0, 1.0, 0.0).astype(F32)
            mask = jnp.where(lane == j, far, 0.0).astype(BF16)
            for p in range(2):
                farl[pl.ds(side * p + CONDUCTORS * j, CONDUCTORS), cols] = pieces[p] * mask
            nearl[pl.ds(CONDUCTORS * j, CONDUCTORS), cols] = rows * jnp.full((CONDUCTORS, TB), 1.0 - far).astype(BF16)
    both = dot(farl[...], rightb[...].reshape(ROWS * TB, TB))
    total = both[:side] + both[side:] + dot(nearl[...], nearb[...].reshape(ROWS * TB, TB))
    for p, piece in enumerate(split(total)):
        wcon[pl.ds(side * p, side), :] = piece.astype(BF16)


def conductor_products(xbuf, wcon):
    total = jnp.zeros((2 * COLS, CONDUCTORS), F32)
    for j in range(TILES):
        xj = stacked(jnp.concatenate([xbuf[2 * j], xbuf[2 * j + 1]], axis=1))
        for p in range(2):
            total = total + dot_nt(xj, wcon[pl.ds(CONDUCTORS * (TILES * p + j), CONDUCTORS), :])
    return total[:COLS] + total[COLS:]


def kernel(
    vol, scal, diag, bnd, cell, lab, left, right, near, slot,
    obuf, bnd_out, charges,
    vbuf, wbuf, qbuf, lhs, sbuf, dbuf, bbuf, cellv, cells, labv, slots, leftb, rightb, nearb,
    xbuf, lbuf, memb, farl, nearl, wcon, ohz, wz, ez, zc, pbuf, rbuf, c1, c2, c3, c4, d1, zsend, zlo, zhi, trbuf,
    load_sem, vol_sem, xs_sem, xr_sem, ls_sem, lr_sem, hs_sem, hr_sem,
    ms_sem, mr_sem, zs_sem, zr_sem, cs_sem, cr_sem, ds_sem, dr_sem, hd_sem, hd_sem2,
):
    gx, gy, gz = lax.axis_index("gx"), lax.axis_index("gy"), lax.axis_index("gz")
    group = (gx * NY + gy) // 2
    pos = lax.rem(gy, 2) * NZ + gz
    own_group = group == gz
    lane = lax.broadcasted_iota(jnp.int32, (COLS, CZ), 1)

    def remote(src, dst, send_sem, recv_sem, device):
        return pltpu.make_async_remote_copy(src, dst, send_sem, recv_sem, device_id=device, device_id_type=MESH)

    def plane(a, b):
        return jnp.bitwise_xor(gx, a), lax.rem(gy + b, NY)

    def line(k):
        return gx, gy, jnp.bitwise_xor(gz, k)

    at_head = jnp.logical_and(gx == HEAD[0], jnp.logical_and(gy == HEAD[1], gz == HEAD[2]))
    away = jnp.logical_not(at_head)
    first = [(jnp.bitwise_xor(gx, a), gy, jnp.bitwise_xor(gz, b)) for a, b in FIRST]
    second = [(jnp.bitwise_xor(gx, 1), lax.rem(gy + b, NY), jnp.bitwise_xor(gz, 2 * c)) for b, c in SECOND]

    small = [(bnd, bbuf), (lab, labv), (cell, cells), (cell, cellv), (slot, slots),
             (scal, sbuf), (diag, dbuf), (right, rightb), (left, leftb), (near, nearb)]
    loads = [pltpu.make_async_copy(s, d, load_sem.at[i]) for i, (s, d) in enumerate(small)]
    (l_bnd, l_lab, l_cells, l_cellv, l_slot, l_scal, l_diag, l_right, l_left, l_near) = loads
    l_bnd.start()
    l_lab.start()

    for x in (0, CX + 1):
        wbuf[x] = jnp.zeros((CY + 2, COLS, CZ), F32)
    for y in (0, CY + 1):
        wbuf[:, y] = jnp.zeros((CX + 2, COLS, CZ), F32)
    zlo[...] = jnp.zeros_like(zlo)
    zhi[...] = jnp.zeros_like(zhi)

    barrier = pltpu.get_barrier_semaphore()

    def greet(device):
        pl.semaphore_signal(barrier, inc=1, device_id=device, device_id_type=MESH)

    for k in LINE + [0]:
        for p in range(2):
            source = (gz // 2, lax.rem(gz, 2) * 2 + p, jnp.bitwise_xor(gz, k))
            if k:
                greet(source)
            else:
                here = jnp.logical_and(own_group, lax.rem(gy, 2) == p)
                pl.when(jnp.logical_not(here))(functools.partial(greet, source))
    for device in second:
        greet(device)
    for k in LINE:
        greet(line(k))
    for device in first:
        greet(device)

    def within(a, b):
        return jnp.logical_and(jnp.logical_and(a >= 0, a < NX), jnp.logical_and(b >= 0, b < NY))

    halo = []
    count = GROUP - own_group.astype(jnp.int32) + len(SECOND) + len(LINE) + len(FIRST)
    for i, (dx, dy) in enumerate(NEIGHBOURS):
        (fx, tx), (fy, ty) = face(dx, CX), face(dy, CY)
        device = (lax.rem(gx + dx + NX, NX), lax.rem(gy + dy + NY, NY), gz)
        to, come = within(gx + dx, gy + dy), within(gx - dx, gy - dy)
        halo.append((remote(wbuf.at[fx, fy], wbuf.at[tx, ty], hs_sem.at[i], hr_sem.at[i], device), to, come))
        pl.when(to)(functools.partial(greet, device))
        count = count + come.astype(jnp.int32)

    @pl.when(at_head)
    def _():
        @pl.loop(0, NX * NY * NZ)
        def _(i):
            device = (i // (NY * NZ), lax.rem(i // NZ, NY), lax.rem(i, NZ))
            pl.when(i != (HEAD[0] * NY + HEAD[1]) * NZ + HEAD[2])(lambda: greet(device))

    count = count + away.astype(jnp.int32)

    l_scal.start()
    for c in range(COLS):
        pltpu.make_async_copy(vol.at[c], vbuf.at[:, c, :], vol_sem).start()
    for l in (l_cells, l_cellv, l_diag, l_slot, l_right, l_left, l_near):
        l.start()
    l_bnd.wait()
    l_lab.wait()
    l_scal.wait()
    pltpu.make_async_copy(vbuf, vbuf, vol_sem).wait()
    scale_pass(sbuf, vbuf, wbuf)
    pl.semaphore_wait(barrier, count)

    x_sends = [remote(bbuf, xbuf.at[pos], xs_sem.at[i], xr_sem, (*plane(a, b), group)) for i, (a, b) in enumerate(PLANE)]
    x_last = remote(bbuf, xbuf.at[pos], xs_sem.at[len(PLANE)], xr_sem, (gx, gy, group))
    x_self = pltpu.make_async_copy(bbuf, xbuf.at[pos], xr_sem)
    label_sends = [remote(labv, lbuf.at[gz], ls_sem, lr_sem, line(k)) for k in LINE]
    for s in x_sends[:2] + label_sends + x_sends[2:]:
        s.start()
    pl.when(jnp.logical_not(own_group))(x_last.start)
    pl.when(own_group)(x_self.start)
    lbuf[gz] = labv[...]

    for copy, to, come in halo:
        pl.when(to)(copy.start)

    l_cells.wait()
    l_cellv.wait()
    l_diag.wait()
    trbuf[...] = trace_nodes(cells, vbuf, lane)
    line_weights(wz, ez)
    node_columns(cellv, ohz)
    node_pass(bbuf, cellv, ohz, vbuf, dbuf, lhs, obuf)
    zsend[...] = jnp.zeros_like(zsend)
    c1[...] = jnp.zeros_like(c1)
    own_sums = conductor_sums(trbuf[...], members(labv[...]))

    pltpu.make_async_copy(lbuf.at[pl.ds(0, NZ - 1)], lbuf.at[pl.ds(0, NZ - 1)], lr_sem).wait()
    for b in range(NZ):
        memb[:, pl.ds(b * BND, BND)] = members(lbuf[b])

    l_slot.wait()
    l_right.wait()
    l_left.wait()
    l_near.wait()
    conductor_weights(memb, slots, rightb, leftb, nearb, farl, nearl, wcon)

    pltpu.make_async_copy(xbuf, xbuf, xr_sem).wait()
    c1[:, pl.ds(0, CONDUCTORS)] = own_sums - conductor_products(xbuf, wcon)
    place = gx * 2 + lax.rem(gz, 2)
    head_place = gy * 4 + gz // 2
    head_send = remote(c1, d1.at[head_place, place], hd_sem, hd_sem2, HEAD)
    pl.when(away)(head_send.start)
    first_sends = [remote(c1, c2.at[place], cs_sem, cr_sem, device) for device in first]
    for s in first_sends:
        s.start()
    c2[place] = c1[...]

    values = tile_products(xbuf, slots, rightb, leftb, nearb)
    for b in range(NZ):
        pbuf[b] = values[:, b * BND:(b + 1) * BND]
    row_sends = [remote(pbuf.at[jnp.bitwise_xor(gz, k)], rbuf.at[gz], ms_sem, mr_sem, line(k)) for k in LINE]
    for s in row_sends:
        s.start()
    rbuf[gz] = pbuf[gz]

    for copy, to, come in halo:
        pl.when(come)(copy.wait_recv)
    line_pass(wbuf, lhs, qbuf)
    sum_pass(lhs, wz, qbuf, sbuf, obuf, zsend, lane)
    up, down = gz + 1 < NZ, gz > 0
    z_up = remote(zsend, zlo, zs_sem.at[0], zr_sem.at[0], (gx, gy, lax.rem(gz + 1, NZ)))
    z_down = remote(zsend, zhi, zs_sem.at[1], zr_sem.at[1], (gx, gy, lax.rem(gz + NZ - 1, NZ)))
    pl.when(up)(z_up.start)
    pl.when(down)(z_down.start)

    pltpu.make_async_copy(c2.at[pl.ds(0, len(FIRST))], c2.at[pl.ds(0, len(FIRST))], cr_sem).wait()
    c3[...] = total_of(c2)
    place = gy * 4 + gz // 2
    second_sends = []
    for i, (device, (b, c)) in enumerate(zip(second, SECOND)):
        to_head = jnp.logical_and(
            jnp.logical_and(gx == HEAD[0] ^ 1, gy == (HEAD[1] - b) % NY), gz == HEAD[2] ^ (2 * c))
        second_sends.append((remote(c3, c4.at[place], ds_sem.at[i], dr_sem, device), jnp.logical_not(to_head)))
    for s, to in second_sends:
        pl.when(to)(s.start)
    c4[place] = c3[...]

    pltpu.make_async_copy(rbuf.at[pl.ds(0, NZ - 1)], rbuf.at[pl.ds(0, NZ - 1)], mr_sem).wait()
    bnd_out[...] = trbuf[...] + total_of(rbuf)
    pl.when(down)(z_up.wait_recv)
    pl.when(up)(z_down.wait_recv)
    end_rows(zlo, zhi, zc, lane)
    end_pass(zc, ez, sbuf, obuf)

    for s in x_sends + label_sends + first_sends + row_sends:
        s.wait_send()
    for s, to in second_sends:
        pl.when(to)(s.wait_send)
    pl.when(away)(head_send.wait_send)
    pl.when(jnp.logical_not(own_group))(x_last.wait_send)
    for copy, to, come in halo:
        pl.when(to)(copy.wait_send)
    pl.when(up)(z_up.wait_send)
    pl.when(down)(z_down.wait_send)

    scale = (CONDUCTORS / (BND * NX * NY * NZ)) ** 0.5

    @pl.when(away)
    def _():
        pltpu.make_async_copy(c4.at[pl.ds(0, len(SECOND))], c4.at[pl.ds(0, len(SECOND))], dr_sem).wait()
        charges[...] = total_of(c4)[:, :CONDUCTORS] * scale

    @pl.when(at_head)
    def _():
        d1[HEAD[1] * 4 + HEAD[2] // 2, HEAD[0] * 2 + HEAD[2] % 2] = c1[...]
        rest = d1.reshape(NX * NY * NZ, COLS, BND).at[pl.ds(0, NX * NY * NZ - 1)]
        pltpu.make_async_copy(rest, rest, hd_sem2).wait()
        for k in range(len(SECOND) + 1):
            c4[k] = total_of(d1.at[k])
        charges[...] = total_of(c4)[:, :CONDUCTORS] * scale


def deliver(field, rows, sums, out, bnd_out, charges, sem, small_sem):
    copies = [pltpu.make_async_copy(field.at[:, c, :], out.at[c], sem) for c in range(COLS)]
    copies.append(pltpu.make_async_copy(rows, bnd_out, small_sem.at[0]))
    copies.append(pltpu.make_async_copy(sums, charges, small_sem.at[1]))
    for c in copies:
        c.start()
    pltpu.make_async_copy(field, field, sem).wait()
    copies[-2].wait()
    copies[-1].wait()


def shards(vol, scal, diag, bnd, cell, lab, left, right, near, slot):
    nodes = CX * CY
    field = (nodes, COLS, CZ)
    dma = pltpu.SemaphoreType.DMA
    hbm_spec = pl.BlockSpec(memory_space=pltpu.HBM)
    vmem_spec = pl.BlockSpec(memory_space=pltpu.VMEM)
    operands = (
        vol.reshape(COLS, nodes, CZ), scal, diag, bnd, cell.reshape(1, BND), lab.reshape(1, BND),
        left.reshape(ROWS, TB, TB), right.reshape(ROWS, TB, TB), near.reshape(ROWS, TB, TB), slot,
    )
    operands = [pltpu.with_memory_space_constraint(o, pltpu.HBM) for o in operands]
    results = pl.pallas_call(
        kernel,
        out_shape=(
            pltpu.VMEM(field, F32),
            pltpu.VMEM((COLS, BND), F32),
            pltpu.VMEM((COLS, CONDUCTORS), F32),
        ),
        in_specs=[hbm_spec] * len(operands),
        out_specs=(vmem_spec,) * 3,
        scratch_shapes=[
            pltpu.VMEM(field, F32),
            pltpu.VMEM((CX + 2, CY + 2, COLS, CZ), F32),
            pltpu.VMEM(field, F32),
            pltpu.VMEM((CX, CY * COLS, 2 * CZ), BF16),
            pltpu.VMEM((CX, CY, CZ), F32),
            pltpu.VMEM((CX, CY, CZ), F32),
            pltpu.VMEM((COLS, BND), F32),
            pltpu.VMEM((1, BND), jnp.int32),
            pltpu.SMEM((1, BND), jnp.int32),
            pltpu.VMEM((1, BND), jnp.int32),
            pltpu.SMEM((ROWS, TILES), jnp.int32),
            pltpu.VMEM((ROWS, TB, TB), BF16),
            pltpu.VMEM((ROWS, TB, TB), BF16),
            pltpu.VMEM((ROWS, TB, TB), BF16),
            pltpu.VMEM((GROUP, COLS, BND), F32),
            pltpu.VMEM((NZ, 1, BND), jnp.int32),
            pltpu.VMEM((CONDUCTORS, NZ * BND), BF16),
            pltpu.VMEM((2 * CONDUCTORS * TILES, ROWS * TB), BF16),
            pltpu.VMEM((CONDUCTORS * TILES, ROWS * TB), BF16),
            pltpu.VMEM((2 * CONDUCTORS * TILES, TB), BF16),
            pltpu.VMEM((CZ, 2 * BND), BF16),
            pltpu.VMEM((2 * CZ, 2 * CZ), BF16),
            pltpu.VMEM((2 * CZ, CZ), BF16),
            pltpu.VMEM((CY * COLS, 2 * CZ), BF16),
            pltpu.VMEM((NZ, COLS, BND), F32),
            pltpu.VMEM((NZ, COLS, BND), F32),
            pltpu.VMEM((COLS, BND), F32),
            pltpu.VMEM((len(FIRST) + 1, COLS, BND), F32),
            pltpu.VMEM((COLS, BND), F32),
            pltpu.VMEM((len(SECOND) + 1, COLS, BND), F32),
            pltpu.VMEM((len(SECOND) + 1, len(FIRST) + 1, COLS, BND), F32),
            pltpu.VMEM((CY // 2, COLS, CZ), F32),
            pltpu.VMEM((CY // 2, COLS, CZ), F32),
            pltpu.VMEM((CY // 2, COLS, CZ), F32),
            pltpu.VMEM((COLS, BND), F32),
            dma((10,)), dma, dma((GROUP,)), dma, dma, dma, dma((8,)), dma((8,)),
            dma, dma, dma((2,)), dma((2,)), dma, dma, dma((len(SECOND),)), dma, dma, dma,
        ],
        compiler_params=pltpu.CompilerParams(
            collective_id=0, has_side_effects=True, vmem_limit_bytes=40 * 1024 * 1024),
    )(*operands)
    out, bnd_out, charges = pl.pallas_call(
        deliver,
        out_shape=(
            pltpu.HBM((COLS, nodes, CZ), F32),
            pltpu.HBM((COLS, BND), F32),
            pltpu.HBM((COLS, CONDUCTORS), F32),
        ),
        in_specs=[vmem_spec] * 3,
        out_specs=(hbm_spec,) * 3,
        scratch_shapes=[dma, dma((2,))],
    )(*[pltpu.with_memory_space_constraint(r, pltpu.VMEM) for r in results])
    return out.reshape(vol.shape), bnd_out, charges.T


def solution(mesh):
    in_specs = (
        P(None, "gx", "gy", "gz"),
        P("gx", "gy", "gz"),
        P("gx", "gy", "gz"),
        P(None, ("gx", "gy", "gz")),
        P(("gx", "gy", "gz")),
        P(("gx", "gy", "gz")),
        P(("gx", "gy"), "gz", None, None),
        P(("gx", "gy"), "gz", None, None),
        P(("gx", "gy"), "gz", None, None),
        P(("gx", "gy"), "gz"),
    )
    out_specs = (P(None, "gx", "gy", "gz"), P(None, ("gx", "gy", "gz")), P())
    return jax.shard_map(shards, mesh=mesh, in_specs=in_specs, out_specs=out_specs, check_vma=False)
```
